32 devices in a mesh: expert: 4 (over x, core), cuts: 8 (over z, y).
Axes of the slice: x: 2, y: 2, z: 4, core: 2. Of those that a mesh axis runs over, the one named last changes fastest.
Arguments:
- out_grad: bfloat16 [256, 3072], P(('expert', 'cuts')), may hold values from -6 to 6
- routes: int32 [256, 2], P(('expert', 'cuts')), may hold values from 0 to 3, all different within a row; in each aligned block of 8 rows (0 to 7, 8 to 15, ...) at most 8 rows name the same one
- gate_weight: float32 [256, 2], P(('expert', 'cuts')), may hold values from 0.1 to 1
- gate_proj: bfloat16 [4, 3072, 16384], P('expert', None, 'cuts'), may hold values from -0.109375 to 0.109375
- up_proj: bfloat16 [4, 3072, 16384], P('expert', None, 'cuts'), may hold values from -0.109375 to 0.109375
- down_proj: bfloat16 [4, 16384, 3072], P('expert', 'cuts'), may hold values from -0.046875 to 0.046875
- saved_gate: bfloat16 [4, 256, 16384], P('expert', None, 'cuts'), may hold values from -6 to 6
- saved_up: bfloat16 [4, 256, 16384], P('expert', None, 'cuts'), may hold values from -6 to 6
Outputs:
- input_grad: bfloat16 [256, 3072], P(('expert', 'cuts'))
The draws below stay inside these ranges and needn't reach their ends.
Inputs may be any that keep to these rules, and one draw needn't show every extreme that they name: `routes`: each token names two different experts. Among the 8 tokens of one device no expert is named more than 8 times, and in some devices one expert is named exactly 8 times.
All inputs are finite; a program needn't handle non-finite values.
Results may differ from the reference program's by a relative error of at most 0.0057.
Values may be sent and summed in bfloat16 or wider, within the bound.
A program may use at most 128 MiB of HBM per device.

```python
import math
import jax
import jax.numpy as jnp
import numpy as np
from jax import lax

D = 3072
FF = 16384
TOK_DEV = 8
EXPERTS = 4
CAP = 8
ROWS = 256
TOKENS = 256
N_EXPERT = 4
N_CUTS = 8


def level_of(own_key, shape, pieces, smallest, top_value):
    level, own = 1.0, jax.random.fold_in(own_key, 6)
    for dim, parts in pieces:
        steps = jnp.exp(jax.random.uniform(jax.random.fold_in(own, dim), (parts,), jnp.float32, smallest / len(pieces), top_value / len(pieces)))
        level = level * jnp.repeat(steps, shape[dim] // parts).reshape([-1 if axis == dim else 1 for axis in range(len(shape))])
    return level


def deal_out(stream_key, own, number, rows, number_of, top, most, lean):
    sequence = jax.random.permutation(stream_key, number_of)
    crowded, usual = load_shares(number_of, rows * top, most, lean, True), load_shares(number_of, rows * top, most, lean, False)
    places = jnp.arange(number_of)

    def named(tallies, offset_by):
        used = int((tallies > 0).sum())
        fixed = max(1, used // 4)
        passed = fixed + (places - fixed + offset_by * (used - fixed)) % max(1, number_of - fixed)
        return jnp.zeros((number_of,), jnp.int32).at[sequence[jnp.where(places < fixed, places, passed)]].set(jnp.asarray(tallies, jnp.int32))

    tallies = jnp.where(number % 4 == 0, named(crowded, number // 4), named(usual, number - number // 4 - 1))
    mixed = jax.random.permutation(jax.random.fold_in(own, 3), number_of)
    giver, taker = mixed[0:number_of // 2 * 2:2], mixed[1:number_of // 2 * 2:2]
    slack = jnp.minimum(tallies[giver] - 1, most - tallies[taker]) // 2
    slack = jnp.where((giver == sequence[0]) | (taker == sequence[0]) | (tallies[taker] == 0), 0, jnp.maximum(slack, 0))
    passed = jax.random.randint(jax.random.fold_in(own, 4), (number_of // 2,), 0, 1 << 20) % (slack + 1)
    tallies = tallies.at[giver].add(-passed).at[taker].add(passed)
    labels = jnp.searchsorted(jnp.cumsum(tallies), jnp.arange(rows * top), side="right").astype(jnp.int32)
    grid = labels.reshape(top, rows).T
    grid = grid[jax.random.permutation(jax.random.fold_in(own, 1), rows)]
    offset_by = jax.random.randint(jax.random.fold_in(own, 2), (rows, 1), 0, top)
    return jnp.take_along_axis(grid, (jnp.arange(top)[None, :] + offset_by) % top, axis=1)


def load_shares(number_of, total, most, slope, full):
    weights = [(1 << 20) // math.isqrt(grade ** slope) + 1 for grade in range(1, number_of + 1)]
    largest = most if full else min(most, max(-(-total // number_of), total * weights[0] // sum(weights)))
    least = 1 if total - largest >= number_of - 1 else 0
    counts, spare = [largest] + [least] * (number_of - 1), total - largest - least * (number_of - 1)
    while spare > 0:
        free = [i for i in range(1, number_of) if counts[i] < largest] or [i for i in range(1, number_of) if counts[i] < most]
        pool, left = sum([weights[i] for i in free]), spare
        for i in free:
            addition = min(most - counts[i], max(1, left * weights[i] // pool), spare)
            counts[i] = counts[i] + addition
            spare = spare - addition
    return np.array(counts)


def bell_draw(key, dims, deviation, limit, split=(), kind=jnp.bfloat16):
    entries = deviation * jax.random.normal(key, dims, jnp.float32)
    if split:
        entries = entries * level_of(key, dims, split, -0.22, 0.18)
    return jnp.clip(entries, -limit, limit).astype(kind)


def setup_inputs(seed: int = 0) -> dict:
    key_list = jax.random.split(jax.random.key(seed), 9)
    out_grad = bell_draw(key_list[0], (TOKENS, D), 1.0, 6.0, ((0, 32),))
    routes_keys = jax.random.split(jax.random.fold_in(key_list[1], 1), TOKENS // TOK_DEV)
    routes_turns = jax.random.permutation(jax.random.fold_in(key_list[1], 3), TOKENS // TOK_DEV)
    routes = jax.vmap(lambda own, number: deal_out(jax.random.fold_in(key_list[1], 2), own, number, TOK_DEV, EXPERTS, 2, CAP, 2))(routes_keys, routes_turns).reshape((TOKENS, 2))
    gate_weight = jnp.clip(0.1 + 0.9 * jax.random.uniform(key_list[2], (TOKENS, 2), jnp.float32) ** level_of(key_list[2], (TOKENS, 2), ((0, 32),), -0.2, 0.2), 0.1, 1.0)
    gate_proj = bell_draw(key_list[3], (EXPERTS, D, FF), D ** -0.5, 0.109375, ((0, 4), (2, 8)))
    up_proj = bell_draw(key_list[4], (EXPERTS, D, FF), D ** -0.5, 0.109375, ((0, 4), (2, 8)))
    down_proj = bell_draw(key_list[5], (EXPERTS, FF, D), FF ** -0.5, 0.046875, ((0, 4), (1, 8)))
    saved_gate = bell_draw(key_list[6], (EXPERTS, ROWS, FF), 1.0, 6.0, ((0, 4), (2, 8)))
    saved_up = bell_draw(key_list[7], (EXPERTS, ROWS, FF), 1.0, 6.0, ((0, 4), (2, 8)))
    return dict(out_grad=out_grad, routes=routes, gate_weight=gate_weight, gate_proj=gate_proj, up_proj=up_proj, down_proj=down_proj, saved_gate=saved_gate, saved_up=saved_up)


def rank_slots(flat_routes):
    count = flat_routes.shape[-1]
    positions = jnp.arange(count, dtype=jnp.int32)
    before = positions[:, None] < positions[None, :]
    matches = flat_routes[..., :, None] == flat_routes[..., None, :]
    return jnp.sum(jnp.logical_and(matches, before), axis=-2).astype(jnp.int32)


def expert_rows(grad_rows, gate_mat, up_mat, down_mat, pre_gate, pre_up):
    contract = (((1,), (1,)), ((), ()))
    hidden_grad = lax.dot_general(grad_rows, down_mat, contract, preferred_element_type=jnp.float32)
    gate_vals = pre_gate.astype(jnp.float32)
    up_vals = pre_up.astype(jnp.float32)
    sigmoid_gate = jax.nn.sigmoid(gate_vals)
    up_grad = (hidden_grad * gate_vals * sigmoid_gate).astype(jnp.bfloat16)
    gate_grad = (hidden_grad * up_vals * sigmoid_gate * (1.0 + gate_vals * (1.0 - sigmoid_gate))).astype(jnp.bfloat16)
    partial_value = lax.dot_general(gate_grad, gate_mat, contract, preferred_element_type=jnp.float32)
    return partial_value + lax.dot_general(up_grad, up_mat, contract, preferred_element_type=jnp.float32)


def reference(out_grad, routes, gate_weight, gate_proj, up_proj, down_proj, saved_gate, saved_up):
    device_count = N_EXPERT * N_CUTS
    block_routes = routes.reshape(device_count, 2 * TOK_DEV)
    slot_index = rank_slots(block_routes)
    device_ids = jnp.arange(device_count, dtype=jnp.int32)
    source_expert = device_ids // N_CUTS
    source_cut = device_ids % N_CUTS
    row_index = (source_cut * N_EXPERT + source_expert)[:, None] * CAP + slot_index
    routed = (gate_weight[:, :, None] * out_grad.astype(jnp.float32)[:, None, :]).astype(jnp.bfloat16)
    routed = routed.reshape(TOKENS * 2, D)
    expert_flat = routes.reshape(-1).astype(jnp.int32)
    row_flat = row_index.reshape(-1).astype(jnp.int32)
    expert_grad = jnp.zeros((EXPERTS, ROWS, D), jnp.bfloat16).at[expert_flat, row_flat].set(routed)
    partial_value = lax.map(lambda items: expert_rows(*items), (expert_grad, gate_proj, up_proj, down_proj, saved_gate, saved_up))
    picked = partial_value[expert_flat, row_flat].reshape(TOKENS, 2, D)
    return jnp.sum(picked, axis=1).astype(jnp.bfloat16)
```

```python
import jax
import jax.numpy as jnp
from jax import lax
from jax.experimental import pallas as pl
from jax.experimental.pallas import tpu as pltpu
from jax.sharding import PartitionSpec as P

MESH = pl.DeviceIdType.MESH
TRANSPOSED = (((1,), (1,)), ((), ()))
META = 128
CHUNK = 512


def fused_kernel(
    tok, routes, gates, gate_hbm, up_hbm, down_hbm, sgate_hbm, sup_hbm, out,
    gate_v, up_v, down_v, sgate_v, sup_v, blocks, rows, gate_g, up_g,
    own, a_send, a_recv, col, b_send, b_recv, c_send, c_recv,
    w_sem, s_sem, gs_sem, gr_sem, as_sem, ar_sem, bs_sem, br_sem, cs_sem, cr_sem,
):
    expert = lax.axis_index("expert")
    cut = lax.axis_index("cuts")
    x, core = expert // 2, expert % 2
    z, y = cut // 2, cut % 2
    feature = tok.shape[1]
    half = feature // 2
    hidden = down_v.shape[0]
    total = rows.shape[0]
    steps = feature // CHUNK
    hidden_steps = hidden // CHUNK

    column = [
        None,
        (expert, z * 2 + (1 - y)),
        ((1 - x) * 2 + core, cut),
        ((1 - x) * 2 + core, z * 2 + (1 - y)),
    ]
    depth = [None] + [(expert, ((z + d) % 4) * 2 + y) for d in (1, 2, 3)]
    twin = (x * 2 + (1 - core), cut)

    def down_copy(n):
        part = pl.ds(pl.multiple_of(n * CHUNK, CHUNK), CHUNK)
        return pltpu.make_async_copy(down_hbm.at[0, part], down_v.at[part], w_sem.at[0, n])

    def gate_copy(n):
        part = pl.ds(pl.multiple_of(n * CHUNK, CHUNK), CHUNK)
        return pltpu.make_async_copy(gate_hbm.at[0, part], gate_v.at[part], w_sem.at[1, n])

    def up_copy(n):
        part = pl.ds(pl.multiple_of(n * CHUNK, CHUNK), CHUNK)
        return pltpu.make_async_copy(up_hbm.at[0, part], up_v.at[part], w_sem.at[2, n])

    saved = [
        pltpu.make_async_copy(sgate_hbm.at[0], sgate_v, s_sem.at[0]),
        pltpu.make_async_copy(sup_hbm.at[0], sup_v, s_sem.at[1]),
    ]

    barrier = pltpu.get_barrier_semaphore()
    for peer in column[1:] + depth[1:] + [twin]:
        pl.semaphore_signal(barrier, inc=1, device_id=peer, device_id_type=MESH)

    for copy in saved:
        copy.start()
    for n in range(hidden_steps):
        down_copy(n).start()
    for n in range(steps):
        gate_copy(n).start()
        up_copy(n).start()

    lane = lax.broadcasted_iota(jnp.int32, (8, META), 1)
    level = lane // 32
    name = lane % 32
    first = (routes[:, 0:1] == name).astype(jnp.float32)
    second = (routes[:, 1:2] == name).astype(jnp.float32)
    hit = first + second
    weight = first * gates[:, 0:1] + second * gates[:, 1:2]
    sub = lax.broadcasted_iota(jnp.int32, (8, META), 0)
    slot = jnp.zeros((8, META), jnp.float32)
    for t in range(7):
        slot = slot + jnp.where(sub > t, hit[t : t + 1, :], 0.0)
    slot = jnp.where(hit > 0.0, slot, -1.0)
    high = weight.astype(jnp.bfloat16).astype(jnp.float32)
    middle = (weight - high).astype(jnp.bfloat16).astype(jnp.float32)
    low = weight - high - middle
    meta = jnp.where(
        level == 0, high, jnp.where(level == 1, middle, jnp.where(level == 2, low, slot))
    )
    tokens = tok[...].astype(jnp.float32)
    stacked = jnp.concatenate([tokens[:, :half], tokens[:, half:]], axis=0)
    blocks[0, :, 0:half] = stacked.astype(jnp.bfloat16)
    blocks[0, :, half : half + META] = jnp.concatenate(
        [meta, jnp.zeros_like(meta)], axis=0
    ).astype(jnp.bfloat16)

    pl.semaphore_wait(barrier, 7)

    def send(source, target, peer, sem):
        copy = pltpu.make_async_remote_copy(
            src_ref=blocks.at[source],
            dst_ref=blocks.at[target],
            send_sem=gs_sem.at[sem],
            recv_sem=gr_sem.at[target],
            device_id=peer,
            device_id_type=MESH,
        )
        copy.start()
        return copy

    def arrived(index):
        pltpu.make_async_remote_copy(
            src_ref=blocks.at[index],
            dst_ref=blocks.at[index],
            send_sem=gs_sem.at[0],
            recv_sem=gr_sem.at[index],
            device_id=twin,
            device_id_type=MESH,
        ).wait_recv()

    sent = []
    for d in (1, 3, 2):
        sent.append(send(0, 4 - d, depth[d], len(sent)))
    for d in (0, 1, 3, 2):
        if d:
            arrived(d)
        for g in (3, 1, 2):
            sent.append(send(d, g * 4 + d, column[g], len(sent)))
        sent.append(send(d, 16 + d, twin, len(sent)))
    for d in (0, 1, 3, 2):
        for g in (1, 2, 3):
            arrived(g * 4 + d)
            sent.append(send(g * 4 + d, 16 + g * 4 + d, twin, len(sent)))
    for d in (0, 1, 3, 2):
        for g in range(4):
            arrived(16 + g * 4 + d)

    info = blocks[:, :, half : half + META].astype(jnp.float32)[:, 0:8, :]
    info = info.reshape(total, META)
    lane = lax.broadcasted_iota(jnp.int32, (total, META), 1)
    mine = (lane % 32) == expert
    weight = jnp.sum(jnp.where(mine & (lane < 96), info, 0.0), axis=1, keepdims=True)
    slot = jnp.sum(jnp.where(mine & (lane >= 96), info, 0.0), axis=1, keepdims=True)
    place = lax.broadcasted_iota(jnp.int32, (total, total), 0)
    far_core = (core + place // 128) % 2
    far_x = (x + (place // 64) % 2) % 2
    far_y = (y + (place // 32) % 2) % 2
    far_z = (z + (place // 8) % 4) % 4
    base = ((far_z * 2 + far_y) * 4 + far_x * 2 + far_core) * 8
    spot = lax.broadcasted_iota(jnp.int32, (total, total), 1) - base
    placing = (spot.astype(jnp.float32) == slot).astype(jnp.bfloat16)

    quarter = half // 4
    for n in range(4):
        part = blocks[:, :, n * quarter : (n + 1) * quarter].astype(jnp.float32)
        for h in range(2):
            value = part[:, h * 8 : h * 8 + 8, :].reshape(total, quarter) * weight
            start = h * half + n * quarter
            rows[:, start : start + quarter] = value.astype(jnp.bfloat16)

    for copy in saved:
        copy.wait()

    @pl.loop(0, hidden_steps)
    def _(n):
        down_copy(n).wait()
        part = pl.ds(pl.multiple_of(n * CHUNK, CHUNK), CHUNK)
        grad = lax.dot_general(
            rows[...], down_v[part, :], TRANSPOSED, preferred_element_type=jnp.float32
        )
        a = jnp.dot(placing, sgate_v[:, part], preferred_element_type=jnp.float32)
        b = jnp.dot(placing, sup_v[:, part], preferred_element_type=jnp.float32)
        q = jax.nn.sigmoid(a)
        up_g[:, part] = (grad * a * q).astype(jnp.bfloat16)
        gate_g[:, part] = (grad * b * q * (1.0 + a * (1.0 - q))).astype(jnp.bfloat16)

    def a_copy(j):
        return pltpu.make_async_remote_copy(
            src_ref=a_send.at[j],
            dst_ref=a_recv.at[j],
            send_sem=as_sem.at[j],
            recv_sem=ar_sem.at[j],
            device_id=twin,
            device_id_type=MESH,
        )

    def b_copy(j, g):
        return pltpu.make_async_remote_copy(
            src_ref=b_send.at[j, g - 1],
            dst_ref=b_recv.at[j, g - 1],
            send_sem=bs_sem.at[j, g - 1],
            recv_sem=br_sem.at[j, g - 1],
            device_id=column[g],
            device_id_type=MESH,
        )

    def c_copy(j, d):
        return pltpu.make_async_remote_copy(
            src_ref=c_send.at[j, d - 1],
            dst_ref=c_recv.at[j, d - 1],
            send_sem=cs_sem.at[j, d - 1],
            recv_sem=cr_sem.at[j, d - 1],
            device_id=depth[d],
            device_id_type=MESH,
        )

    @pl.loop(0, steps + 3)
    def _(i):
        @pl.when(i < steps)
        def _():
            gate_copy(i).wait()
            up_copy(i).wait()
            part = pl.ds(pl.multiple_of(i * CHUNK, CHUNK), CHUNK)
            value = lax.dot_general(
                gate_g[...], gate_v[part, :], TRANSPOSED, preferred_element_type=jnp.float32
            ) + lax.dot_general(
                up_g[...], up_v[part, :], TRANSPOSED, preferred_element_type=jnp.float32
            )
            a_send[i] = value[128:256].astype(jnp.bfloat16)
            own[i] = value[0:128]
            a_copy(i).start()

        @pl.when((i >= 1) & (i < steps + 1))
        def _():
            j = i - 1
            a_copy(j).wait_recv()
            value = own[j] + a_recv[j].astype(jnp.float32)
            for g in (3, 1, 2):
                b_send[j, g - 1] = value[g * 32 : g * 32 + 32].astype(jnp.bfloat16)
                b_copy(j, g).start()
            col[j] = value[0:32]

        @pl.when((i >= 2) & (i < steps + 2))
        def _():
            j = i - 2
            value = col[j]
            for g in (1, 2, 3):
                b_copy(j, g).wait_recv()
                value = value + b_recv[j, g - 1].astype(jnp.float32)
            for d in (2, 1, 3):
                line = value[d * 8 : d * 8 + 8]
                folded = jnp.concatenate([line[:, : CHUNK // 2], line[:, CHUNK // 2 :]], axis=0)
                c_send[j, d - 1] = folded.astype(jnp.bfloat16)
                c_copy(j, d).start()
            col[j, 0:8, :] = value[0:8]

        @pl.when(i >= 3)
        def _():
            j = i - 3
            value = col[j, 0:8, :]
            for d in (1, 2, 3):
                c_copy(j, d).wait_recv()
                folded = c_recv[j, d - 1].astype(jnp.float32)
                value = value + jnp.concatenate([folded[0:8], folded[8:16]], axis=1)
            part = pl.ds(pl.multiple_of(j * CHUNK, CHUNK), CHUNK)
            out[:, part] = value.astype(out.dtype)

    for copy in sent:
        copy.wait_send()

    @pl.loop(0, steps)
    def _(j):
        a_copy(j).wait_send()
        for g in (1, 2, 3):
            b_copy(j, g).wait_send()
        for d in (1, 2, 3):
            c_copy(j, d).wait_send()


def fused_shards(out_grad, routes, gate_weight, gate_proj, up_proj, down_proj, saved_gate, saved_up):
    feature = out_grad.shape[1]
    hidden = gate_proj.shape[2]
    total = saved_gate.shape[1]
    steps = feature // CHUNK
    bf16, f32 = jnp.bfloat16, jnp.float32
    vmem = pl.BlockSpec(memory_space=pltpu.VMEM)
    anywhere = pl.BlockSpec(memory_space=pl.ANY)
    dma = pltpu.SemaphoreType.DMA
    flops = 2 * 3 * total * feature * hidden
    return pl.pallas_call(
        fused_kernel,
        out_shape=jax.ShapeDtypeStruct(out_grad.shape, bf16),
        in_specs=[vmem] * 3 + [anywhere] * 5,
        out_specs=vmem,
        scratch_shapes=[
            pltpu.VMEM((feature, hidden), bf16),
            pltpu.VMEM((feature, hidden), bf16),
            pltpu.VMEM((hidden, feature), bf16),
            pltpu.VMEM((total, hidden), bf16),
            pltpu.VMEM((total, hidden), bf16),
            pltpu.VMEM((32, 16, feature // 2 + META), bf16),
            pltpu.VMEM((total, feature), bf16),
            pltpu.VMEM((total, hidden), bf16),
            pltpu.VMEM((total, hidden), bf16),
            pltpu.VMEM((steps, 128, CHUNK), f32),
            pltpu.VMEM((steps, 128, CHUNK), bf16),
            pltpu.VMEM((steps, 128, CHUNK), bf16),
            pltpu.VMEM((steps, 32, CHUNK), f32),
            pltpu.VMEM((steps, 3, 32, CHUNK), bf16),
            pltpu.VMEM((steps, 3, 32, CHUNK), bf16),
            pltpu.VMEM((steps, 3, 16, CHUNK // 2), bf16),
            pltpu.VMEM((steps, 3, 16, CHUNK // 2), bf16),
            dma((3, max(steps, hidden // CHUNK))),
            dma((2,)),
            dma((31,)),
            dma((32,)),
            dma((steps,)),
            dma((steps,)),
            dma((steps, 3)),
            dma((steps, 3)),
            dma((steps, 3)),
            dma((steps, 3)),
        ],
        compiler_params=pltpu.CompilerParams(
            collective_id=0, has_side_effects=True, vmem_limit_bytes=60 * 1024 * 1024
        ),
        cost_estimate=pl.CostEstimate(
            flops=flops, bytes_accessed=3 * 2 * feature * hidden, transcendentals=total * hidden
        ),
    )(out_grad, routes, gate_weight, gate_proj, up_proj, down_proj, saved_gate, saved_up)


def rank_slots(flat_routes):
    count = flat_routes.shape[-1]
    positions = jnp.arange(count, dtype=jnp.int32)
    before = positions[:, None] < positions[None, :]
    matches = flat_routes[..., :, None] == flat_routes[..., None, :]
    return jnp.sum(jnp.logical_and(matches, before), axis=-2)


def expert_rows(grad_rows, gate_mat, up_mat, down_mat, pre_gate, pre_up):
    contract = (((1,), (1,)), ((), ()))
    hidden_grad = lax.dot_general(grad_rows, down_mat, contract, preferred_element_type=jnp.float32)
    gate_vals = pre_gate.astype(jnp.float32)
    up_vals = pre_up.astype(jnp.float32)
    sigmoid_gate = jax.nn.sigmoid(gate_vals)
    up_grad = (hidden_grad * gate_vals * sigmoid_gate).astype(jnp.bfloat16)
    gate_grad = (
        hidden_grad * up_vals * sigmoid_gate * (1.0 + gate_vals * (1.0 - sigmoid_gate))
    ).astype(jnp.bfloat16)
    partial_value = lax.dot_general(
        gate_grad, gate_mat, contract, preferred_element_type=jnp.float32
    )
    return partial_value + lax.dot_general(
        up_grad, up_mat, contract, preferred_element_type=jnp.float32
    )


def shards(out_grad, routes, gate_weight, gate_proj, up_proj, down_proj, saved_gate, saved_up):
    expert_count = lax.axis_size("expert")
    cut_count = lax.axis_size("cuts")
    tok_rows = out_grad.shape[0]
    feature_dim = out_grad.shape[1]
    slot_count = saved_gate.shape[1] // (expert_count * cut_count)
    flat_routes = routes.reshape(-1)
    slot_index = rank_slots(flat_routes[None, :])[0]
    own_spots = flat_routes * slot_count + slot_index
    routed = (gate_weight[:, :, None] * out_grad.astype(jnp.float32)[:, None, :]).astype(
        jnp.bfloat16
    )
    routed = routed.reshape(2 * tok_rows, feature_dim)
    places = jnp.arange(expert_count * slot_count, dtype=jnp.int32)
    placing = (places[:, None] == own_spots[None, :]).astype(jnp.bfloat16)
    outgoing = jnp.dot(placing, routed, preferred_element_type=jnp.float32).astype(jnp.bfloat16)
    outgoing = outgoing.reshape(expert_count, slot_count, feature_dim)
    arrived = lax.all_to_all(outgoing, "expert", split_axis=0, concat_axis=0, tiled=True)
    gathered = lax.all_gather(arrived, "cuts", axis=0, tiled=True).reshape(-1, feature_dim)
    gate_block = saved_gate[0]
    up_block = saved_up[0]
    own_rows = lax.psum_scatter(
        expert_rows(gathered, gate_proj[0], up_proj[0], down_proj[0], gate_block, up_block),
        "cuts",
        scatter_dimension=0,
        tiled=True,
    )
    own_rows = own_rows.reshape(expert_count, slot_count, feature_dim)
    returned = lax.all_to_all(own_rows, "expert", split_axis=0, concat_axis=0, tiled=True).reshape(
        -1, feature_dim
    )
    picked = returned[own_spots].reshape(tok_rows, 2, feature_dim)
    summed = jnp.sum(picked, axis=1)
    return summed.astype(jnp.bfloat16)


def solution(mesh):
    in_specs = (
        P(("expert", "cuts"), None),
        P(("expert", "cuts"), None),
        P(("expert", "cuts"), None),
        P("expert", None, "cuts"),
        P("expert", None, "cuts"),
        P("expert", "cuts", None),
        P("expert", None, "cuts"),
        P("expert", None, "cuts"),
    )
    out_specs = P(("expert", "cuts"), None)
    fused = (mesh.shape["expert"], mesh.shape["cuts"]) == (4, 8)
    body = fused_shards if fused else shards
    return jax.shard_map(body, mesh=mesh, in_specs=in_specs, out_specs=out_specs, check_vma=False)
```

```python
import jax
import jax.numpy as jnp
from jax import lax
from jax.experimental import pallas as pl
from jax.experimental.pallas import tpu as pltpu
from jax.sharding import PartitionSpec as P

MESH = pl.DeviceIdType.MESH
LEADING = (((0,), (0,)), ((), ()))
META = 128
CHUNK = 512


def upright(ref, choice):
    across = jnp.broadcast_to(ref[choice : choice + 1, :].astype(jnp.float32), (8, 8))
    keep = lax.broadcasted_iota(jnp.int32, (8, 8), 0) == lax.broadcasted_iota(jnp.int32, (8, 8), 1)
    return jnp.sum(jnp.where(keep, across, 0.0), axis=1, keepdims=True)


def fused_kernel(
    tok, routes, gates, gate_hbm, up_hbm, down_hbm, sgate_hbm, sup_hbm, out,
    gate_v, up_v, down_v, sgate_v, sup_v, blocks, rows, gate_g, up_g,
    own, a_send, a_recv, col, b_send, b_recv, c_send, c_recv,
    w_sem, s_sem, gs_sem, gr_sem, as_sem, ar_sem, bs_sem, br_sem, cs_sem, cr_sem,
):
    expert = lax.axis_index("expert")
    cut = lax.axis_index("cuts")
    x, core = expert // 2, expert % 2
    z, y = cut // 2, cut % 2
    feature = tok.shape[1]
    half = feature // 2
    hidden = down_v.shape[0]
    total = rows.shape[1]
    steps = feature // CHUNK
    hidden_steps = hidden // CHUNK

    column = [
        None,
        (expert, z * 2 + (1 - y)),
        ((1 - x) * 2 + core, cut),
        ((1 - x) * 2 + core, z * 2 + (1 - y)),
    ]
    z_high, z_low = z // 2, z % 2
    depth = [None] + [
        (expert, (((z_high + d // 2) % 2) * 2 + (z_low + d % 2) % 2) * 2 + y) for d in (1, 2, 3)
    ]
    twin = (x * 2 + (1 - core), cut)

    def down_copy(n):
        part = pl.ds(pl.multiple_of(n * CHUNK, CHUNK), CHUNK)
        return pltpu.make_async_copy(down_hbm.at[0, part], down_v.at[part], w_sem.at[0, n])

    def gate_copy(n):
        part = pl.ds(pl.multiple_of(n * CHUNK, CHUNK), CHUNK)
        return pltpu.make_async_copy(gate_hbm.at[0, part], gate_v.at[part], w_sem.at[1, n])

    def up_copy(n):
        part = pl.ds(pl.multiple_of(n * CHUNK, CHUNK), CHUNK)
        return pltpu.make_async_copy(up_hbm.at[0, part], up_v.at[part], w_sem.at[2, n])

    saved = [
        pltpu.make_async_copy(sgate_hbm.at[0], sgate_v, s_sem.at[0]),
        pltpu.make_async_copy(sup_hbm.at[0], sup_v, s_sem.at[1]),
    ]

    barrier = pltpu.get_barrier_semaphore()
    for peer in column[1:] + depth[1:] + [twin]:
        pl.semaphore_signal(barrier, inc=1, device_id=peer, device_id_type=MESH)

    for copy in saved:
        copy.start()
    for n in range(hidden_steps):
        down_copy(n).start()
    for n in range(steps):
        gate_copy(n).start()
        up_copy(n).start()

    lane = lax.broadcasted_iota(jnp.int32, (8, META), 1)
    level = lane // 32
    name = lane % 32
    first = (upright(routes, 0) == name.astype(jnp.float32)).astype(jnp.float32)
    second = (upright(routes, 1) == name.astype(jnp.float32)).astype(jnp.float32)
    hit = first + second
    weight = first * upright(gates, 0) + second * upright(gates, 1)
    sub = lax.broadcasted_iota(jnp.int32, (8, META), 0)
    slot = jnp.zeros((8, META), jnp.float32)
    for t in range(7):
        slot = slot + jnp.where(sub > t, hit[t : t + 1, :], 0.0)
    slot = jnp.where(hit > 0.0, slot, -1.0)
    high = weight.astype(jnp.bfloat16).astype(jnp.float32)
    middle = (weight - high).astype(jnp.bfloat16).astype(jnp.float32)
    low = weight - high - middle
    meta = jnp.where(
        level == 0, high, jnp.where(level == 1, middle, jnp.where(level == 2, low, slot))
    )
    tokens = tok[...].astype(jnp.float32)
    stacked = jnp.concatenate([tokens[:, :half], tokens[:, half:]], axis=0)
    blocks[0, :, 0:half] = stacked.astype(jnp.bfloat16)
    blocks[0, :, half : half + META] = jnp.concatenate(
        [meta, jnp.zeros_like(meta)], axis=0
    ).astype(jnp.bfloat16)

    pl.semaphore_wait(barrier, 7)

    def send(source, target, peer, sem):
        copy = pltpu.make_async_remote_copy(
            src_ref=blocks.at[source],
            dst_ref=blocks.at[target],
            send_sem=gs_sem.at[sem],
            recv_sem=gr_sem.at[target],
            device_id=peer,
            device_id_type=MESH,
        )
        copy.start()
        return copy

    def arrived(index):
        pltpu.make_async_remote_copy(
            src_ref=blocks.at[index],
            dst_ref=blocks.at[index],
            send_sem=gs_sem.at[0],
            recv_sem=gr_sem.at[index],
            device_id=twin,
            device_id_type=MESH,
        ).wait_recv()

    sent = []
    order = (0, 2, 1, 3)
    for d in (2, 1, 3):
        sent.append(send(0, d, depth[d], len(sent)))
    for d in order:
        if d:
            arrived(d)
        for g in (3, 1, 2) if d in (0, 2) else (1, 2):
            sent.append(send(d, g * 4 + d, column[g], len(sent)))
        sent.append(send(d, 16 + d, twin, len(sent)))
        if d == 1:
            arrived(12)
            sent.append(send(12, 13, depth[1], len(sent)))
            sent.append(send(12, 28, twin, len(sent)))
    arrived(14)
    sent.append(send(14, 15, depth[1], len(sent)))
    sent.append(send(14, 30, twin, len(sent)))
    for d in order:
        for g in (1, 2):
            arrived(g * 4 + d)
            sent.append(send(g * 4 + d, 16 + g * 4 + d, twin, len(sent)))
    for d in (1, 3):
        arrived(12 + d)
        sent.append(send(12 + d, 28 + d, twin, len(sent)))
    for d in order:
        for g in range(4):
            arrived(16 + g * 4 + d)

    info = blocks[:, :, half : half + META].astype(jnp.float32)[:, 0:8, :]
    info = info.reshape(total, META)
    lane = lax.broadcasted_iota(jnp.int32, (total, META), 1)
    mine = (lane % 32) == expert
    weight = jnp.sum(jnp.where(mine & (lane < 96), info, 0.0), axis=1, keepdims=True)
    slot = jnp.sum(jnp.where(mine & (lane >= 96), info, 0.0), axis=1, keepdims=True)
    place = lax.broadcasted_iota(jnp.int32, (total, total), 0)
    far_core = (core + place // 128) % 2
    far_x = (x + (place // 64) % 2) % 2
    far_y = (y + (place // 32) % 2) % 2
    far_z = ((z_high + (place // 16) % 2) % 2) * 2 + (z_low + (place // 8) % 2) % 2
    base = ((far_z * 2 + far_y) * 4 + far_x * 2 + far_core) * 8
    spot = lax.broadcasted_iota(jnp.int32, (total, total), 1) - base
    placing = (spot.astype(jnp.float32) == slot).astype(jnp.float32).T.astype(jnp.bfloat16)

    quarter = half // 4
    for n in range(4):
        part = blocks[:, :, n * quarter : (n + 1) * quarter].astype(jnp.float32)
        for h in range(2):
            value = part[:, h * 8 : h * 8 + 8, :].reshape(total, quarter) * weight
            start = h * half + n * quarter
            rows[start : start + quarter, :] = value.astype(jnp.bfloat16).T

    for copy in saved:
        copy.wait()

    @pl.loop(0, hidden_steps)
    def _(n):
        down_copy(n).wait()
        part = pl.ds(pl.multiple_of(n * CHUNK, CHUNK), CHUNK)
        grad = jnp.dot(down_v[part, :], rows[...], preferred_element_type=jnp.float32)
        a = lax.dot_general(
            sgate_v[:, part], placing, LEADING, preferred_element_type=jnp.float32
        )
        b = lax.dot_general(sup_v[:, part], placing, LEADING, preferred_element_type=jnp.float32)
        q = jax.nn.sigmoid(a)
        up_g[part, :] = (grad * a * q).astype(jnp.bfloat16)
        gate_g[part, :] = (grad * b * q * (1.0 + a * (1.0 - q))).astype(jnp.bfloat16)

    def a_copy(j):
        return pltpu.make_async_remote_copy(
            src_ref=a_send.at[j],
            dst_ref=a_recv.at[j],
            send_sem=as_sem.at[j],
            recv_sem=ar_sem.at[j],
            device_id=twin,
            device_id_type=MESH,
        )

    def b_copy(j, g):
        return pltpu.make_async_remote_copy(
            src_ref=b_send.at[j, g - 1],
            dst_ref=b_recv.at[j, g - 1],
            send_sem=bs_sem.at[j, g - 1],
            recv_sem=br_sem.at[j, g - 1],
            device_id=column[g],
            device_id_type=MESH,
        )

    def c_copy(j, d):
        return pltpu.make_async_remote_copy(
            src_ref=c_send.at[j, d - 1],
            dst_ref=c_recv.at[j, d - 1],
            send_sem=cs_sem.at[j, d - 1],
            recv_sem=cr_sem.at[j, d - 1],
            device_id=depth[d],
            device_id_type=MESH,
        )

    @pl.loop(0, steps + 3)
    def _(i):
        @pl.when(i < steps)
        def _():
            gate_copy(i).wait()
            up_copy(i).wait()
            part = pl.ds(pl.multiple_of(i * CHUNK, CHUNK), CHUNK)
            value = jnp.dot(
                gate_v[part, :], gate_g[...], preferred_element_type=jnp.float32
            ) + jnp.dot(up_v[part, :], up_g[...], preferred_element_type=jnp.float32)
            value = value.T
            a_send[i] = value[128:256].astype(jnp.bfloat16)
            own[i] = value[0:128]
            a_copy(i).start()

        @pl.when((i >= 1) & (i < steps + 1))
        def _():
            j = i - 1
            a_copy(j).wait_recv()
            value = own[j] + a_recv[j].astype(jnp.float32)
            for g in (3, 1, 2):
                b_send[j, g - 1] = value[g * 32 : g * 32 + 32].astype(jnp.bfloat16)
                b_copy(j, g).start()
            col[j] = value[0:32]

        @pl.when((i >= 2) & (i < steps + 2))
        def _():
            j = i - 2
            value = col[j]
            for g in (1, 2, 3):
                b_copy(j, g).wait_recv()
                value = value + b_recv[j, g - 1].astype(jnp.float32)
            for d in (2, 1, 3):
                line = value[d * 8 : d * 8 + 8]
                folded = jnp.concatenate([line[:, : CHUNK // 2], line[:, CHUNK // 2 :]], axis=0)
                c_send[j, d - 1] = folded.astype(jnp.bfloat16)
                c_copy(j, d).start()
            col[j, 0:8, :] = value[0:8]

        @pl.when(i >= 3)
        def _():
            j = i - 3
            value = col[j, 0:8, :]
            for d in (1, 2, 3):
                c_copy(j, d).wait_recv()
                folded = c_recv[j, d - 1].astype(jnp.float32)
                value = value + jnp.concatenate([folded[0:8], folded[8:16]], axis=1)
            part = pl.ds(pl.multiple_of(j * CHUNK, CHUNK), CHUNK)
            out[:, part] = value.astype(out.dtype)

    for copy in sent:
        copy.wait_send()

    @pl.loop(0, steps)
    def _(j):
        a_copy(j).wait_send()
        for g in (1, 2, 3):
            b_copy(j, g).wait_send()
        for d in (1, 2, 3):
            c_copy(j, d).wait_send()


def fused_shards(out_grad, routes, gate_weight, gate_proj, up_proj, down_proj, saved_gate, saved_up):
    feature = out_grad.shape[1]
    hidden = gate_proj.shape[2]
    total = saved_gate.shape[1]
    steps = feature // CHUNK
    bf16, f32 = jnp.bfloat16, jnp.float32
    vmem = pl.BlockSpec(memory_space=pltpu.VMEM)
    anywhere = pl.BlockSpec(memory_space=pl.ANY)
    dma = pltpu.SemaphoreType.DMA
    flops = 2 * 3 * total * feature * hidden
    return pl.pallas_call(
        fused_kernel,
        out_shape=jax.ShapeDtypeStruct(out_grad.shape, bf16),
        in_specs=[vmem] * 3 + [anywhere] * 5,
        out_specs=vmem,
        scratch_shapes=[
            pltpu.VMEM((feature, hidden), bf16),
            pltpu.VMEM((feature, hidden), bf16),
            pltpu.VMEM((hidden, feature), bf16),
            pltpu.VMEM((total, hidden), bf16),
            pltpu.VMEM((total, hidden), bf16),
            pltpu.VMEM((32, 16, feature // 2 + META), bf16),
            pltpu.VMEM((feature, total), bf16),
            pltpu.VMEM((hidden, total), bf16),
            pltpu.VMEM((hidden, total), bf16),
            pltpu.VMEM((steps, 128, CHUNK), f32),
            pltpu.VMEM((steps, 128, CHUNK), bf16),
            pltpu.VMEM((steps, 128, CHUNK), bf16),
            pltpu.VMEM((steps, 32, CHUNK), f32),
            pltpu.VMEM((steps, 3, 32, CHUNK), bf16),
            pltpu.VMEM((steps, 3, 32, CHUNK), bf16),
            pltpu.VMEM((steps, 3, 16, CHUNK // 2), bf16),
            pltpu.VMEM((steps, 3, 16, CHUNK // 2), bf16),
            dma((3, max(steps, hidden // CHUNK))),
            dma((2,)),
            dma((31,)),
            dma((32,)),
            dma((steps,)),
            dma((steps,)),
            dma((steps, 3)),
            dma((steps, 3)),
            dma((steps, 3)),
            dma((steps, 3)),
        ],
        compiler_params=pltpu.CompilerParams(
            collective_id=0, has_side_effects=True, vmem_limit_bytes=60 * 1024 * 1024
        ),
        cost_estimate=pl.CostEstimate(
            flops=flops, bytes_accessed=3 * 2 * feature * hidden, transcendentals=total * hidden
        ),
    )(out_grad, routes.T, gate_weight.T, gate_proj, up_proj, down_proj, saved_gate, saved_up)


def rank_slots(flat_routes):
    count = flat_routes.shape[-1]
    positions = jnp.arange(count, dtype=jnp.int32)
    before = positions[:, None] < positions[None, :]
    matches = flat_routes[..., :, None] == flat_routes[..., None, :]
    return jnp.sum(jnp.logical_and(matches, before), axis=-2)


def expert_rows(grad_rows, gate_mat, up_mat, down_mat, pre_gate, pre_up):
    contract = (((1,), (1,)), ((), ()))
    hidden_grad = lax.dot_general(grad_rows, down_mat, contract, preferred_element_type=jnp.float32)
    gate_vals = pre_gate.astype(jnp.float32)
    up_vals = pre_up.astype(jnp.float32)
    sigmoid_gate = jax.nn.sigmoid(gate_vals)
    up_grad = (hidden_grad * gate_vals * sigmoid_gate).astype(jnp.bfloat16)
    gate_grad = (
        hidden_grad * up_vals * sigmoid_gate * (1.0 + gate_vals * (1.0 - sigmoid_gate))
    ).astype(jnp.bfloat16)
    partial_value = lax.dot_general(
        gate_grad, gate_mat, contract, preferred_element_type=jnp.float32
    )
    return partial_value + lax.dot_general(
        up_grad, up_mat, contract, preferred_element_type=jnp.float32
    )


def shards(out_grad, routes, gate_weight, gate_proj, up_proj, down_proj, saved_gate, saved_up):
    expert_count = lax.axis_size("expert")
    cut_count = lax.axis_size("cuts")
    tok_rows = out_grad.shape[0]
    feature_dim = out_grad.shape[1]
    slot_count = saved_gate.shape[1] // (expert_count * cut_count)
    flat_routes = routes.reshape(-1)
    slot_index = rank_slots(flat_routes[None, :])[0]
    own_spots = flat_routes * slot_count + slot_index
    routed = (gate_weight[:, :, None] * out_grad.astype(jnp.float32)[:, None, :]).astype(
        jnp.bfloat16
    )
    routed = routed.reshape(2 * tok_rows, feature_dim)
    places = jnp.arange(expert_count * slot_count, dtype=jnp.int32)
    placing = (places[:, None] == own_spots[None, :]).astype(jnp.bfloat16)
    outgoing = jnp.dot(placing, routed, preferred_element_type=jnp.float32).astype(jnp.bfloat16)
    outgoing = outgoing.reshape(expert_count, slot_count, feature_dim)
    arrived = lax.all_to_all(outgoing, "expert", split_axis=0, concat_axis=0, tiled=True)
    gathered = lax.all_gather(arrived, "cuts", axis=0, tiled=True).reshape(-1, feature_dim)
    gate_block = saved_gate[0]
    up_block = saved_up[0]
    own_rows = lax.psum_scatter(
        expert_rows(gathered, gate_proj[0], up_proj[0], down_proj[0], gate_block, up_block),
        "cuts",
        scatter_dimension=0,
        tiled=True,
    )
    own_rows = own_rows.reshape(expert_count, slot_count, feature_dim)
    returned = lax.all_to_all(own_rows, "expert", split_axis=0, concat_axis=0, tiled=True).reshape(
        -1, feature_dim
    )
    picked = returned[own_spots].reshape(tok_rows, 2, feature_dim)
    summed = jnp.sum(picked, axis=1)
    return summed.astype(jnp.bfloat16)


def solution(mesh):
    in_specs = (
        P(("expert", "cuts"), None),
        P(("expert", "cuts"), None),
        P(("expert", "cuts"), None),
        P("expert", None, "cuts"),
        P("expert", None, "cuts"),
        P("expert", "cuts", None),
        P("expert", None, "cuts"),
        P("expert", None, "cuts"),
    )
    out_specs = P(("expert", "cuts"), None)
    fused = (mesh.shape["expert"], mesh.shape["cuts"]) == (4, 8)
    body = fused_shards if fused else shards
    return jax.shard_map(body, mesh=mesh, in_specs=in_specs, out_specs=out_specs, check_vma=False)
```

```python
import jax
import jax.numpy as jnp
from jax import lax
from jax.experimental import pallas as pl
from jax.experimental.pallas import tpu as pltpu
from jax.sharding import PartitionSpec as P

MESH = pl.DeviceIdType.MESH
LEADING = (((0,), (0,)), ((), ()))
META = 128
CHUNK = 512


def upright(ref, choice):
    across = jnp.broadcast_to(ref[choice : choice + 1, :].astype(jnp.float32), (8, 8))
    keep = lax.broadcasted_iota(jnp.int32, (8, 8), 0) == lax.broadcasted_iota(jnp.int32, (8, 8), 1)
    return jnp.sum(jnp.where(keep, across, 0.0), axis=1, keepdims=True)


def fused_kernel(
    tok, routes, gates, gate_hbm, up_hbm, down_hbm, sgate_hbm, sup_hbm, out,
    gate_v, up_v, down_v, sgate_v, sup_v, blocks, meta, rows, gate_g, up_g, gate_f, up_f,
    own, a_send, a_recv, col, b_send, b_recv, c_send, c_recv,
    w_sem, s_sem, ms_sem, mr_sem, gs_sem, gr_sem, as_sem, ar_sem, bs_sem, br_sem, cs_sem, cr_sem,
):
    expert = lax.axis_index("expert")
    cut = lax.axis_index("cuts")
    x, core = expert // 2, expert % 2
    z, y = cut // 2, cut % 2
    feature = tok.shape[1]
    half = feature // 2
    hidden = down_v.shape[0]
    total = rows.shape[1]
    steps = feature // CHUNK
    hidden_steps = hidden // CHUNK

    column = [
        None,
        (expert, z * 2 + (1 - y)),
        ((1 - x) * 2 + core, cut),
        ((1 - x) * 2 + core, z * 2 + (1 - y)),
    ]
    z_high, z_low = z // 2, z % 2
    depth = [None] + [
        (expert, (((z_high + d // 2) % 2) * 2 + (z_low + d % 2) % 2) * 2 + y) for d in (1, 2, 3)
    ]
    twin = (x * 2 + (1 - core), cut)

    def down_copy(n):
        part = pl.ds(pl.multiple_of(n * CHUNK, CHUNK), CHUNK)
        return pltpu.make_async_copy(down_hbm.at[0, part], down_v.at[part], w_sem.at[0, n])

    def gate_copy(n):
        part = pl.ds(pl.multiple_of(n * CHUNK, CHUNK), CHUNK)
        return pltpu.make_async_copy(gate_hbm.at[0, part], gate_v.at[part], w_sem.at[1, n])

    def up_copy(n):
        part = pl.ds(pl.multiple_of(n * CHUNK, CHUNK), CHUNK)
        return pltpu.make_async_copy(up_hbm.at[0, part], up_v.at[part], w_sem.at[2, n])

    saved = [
        pltpu.make_async_copy(sgate_hbm.at[0], sgate_v, s_sem.at[0]),
        pltpu.make_async_copy(sup_hbm.at[0], sup_v, s_sem.at[1]),
    ]

    barrier = pltpu.get_barrier_semaphore()
    for peer in column[1:] + depth[1:] + [twin]:
        pl.semaphore_signal(barrier, inc=1, device_id=peer, device_id_type=MESH)

    for copy in saved:
        copy.start()
    for n in range(hidden_steps):
        down_copy(n).start()

    lane = lax.broadcasted_iota(jnp.int32, (8, META), 1)
    level = lane // 32
    name = lane % 32
    first = (upright(routes, 0) == name.astype(jnp.float32)).astype(jnp.float32)
    second = (upright(routes, 1) == name.astype(jnp.float32)).astype(jnp.float32)
    hit = first + second
    weight = first * upright(gates, 0) + second * upright(gates, 1)
    sub = lax.broadcasted_iota(jnp.int32, (8, META), 0)
    slot = jnp.zeros((8, META), jnp.float32)
    for t in range(7):
        slot = slot + jnp.where(sub > t, hit[t : t + 1, :], 0.0)
    slot = jnp.where(hit > 0.0, slot, -1.0)
    high = weight.astype(jnp.bfloat16).astype(jnp.float32)
    middle = (weight - high).astype(jnp.bfloat16).astype(jnp.float32)
    low = weight - high - middle
    routing = jnp.where(
        level == 0, high, jnp.where(level == 1, middle, jnp.where(level == 2, low, slot))
    )
    meta[0] = jnp.concatenate([routing, jnp.zeros_like(routing)], axis=0).astype(jnp.bfloat16)
    tokens = tok[...].astype(jnp.float32)
    stacked = jnp.concatenate([tokens[:, :half], tokens[:, half:]], axis=0)
    blocks[0] = stacked.astype(jnp.bfloat16)

    pl.semaphore_wait(barrier, 7)

    def send(source, target, peer, sem):
        copy = pltpu.make_async_remote_copy(
            src_ref=blocks.at[source],
            dst_ref=blocks.at[target],
            send_sem=gs_sem.at[sem],
            recv_sem=gr_sem.at[target],
            device_id=peer,
            device_id_type=MESH,
        )
        copy.start()
        return copy

    def arrived(index):
        pltpu.make_async_remote_copy(
            src_ref=blocks.at[index],
            dst_ref=blocks.at[index],
            send_sem=gs_sem.at[0],
            recv_sem=gr_sem.at[index],
            device_id=twin,
            device_id_type=MESH,
        ).wait_recv()

    sent = []
    def meta_copy(n, source, target, count, peer):
        return pltpu.make_async_remote_copy(
            src_ref=meta.at[pl.ds(source, count)],
            dst_ref=meta.at[pl.ds(target, count)],
            send_sem=ms_sem.at[n],
            recv_sem=mr_sem.at[n],
            device_id=peer,
            device_id_type=MESH,
        )

    meta_depth = [meta_copy(d - 1, 0, d, 1, depth[d]) for d in (1, 2, 3)]
    meta_column = [meta_copy(2 + g, 0, g * 4, 4, column[g]) for g in (1, 2, 3)]
    meta_twin = meta_copy(6, 0, 16, 16, twin)

    def to_twin(index):
        sent.append(send(index, 16 + index, twin, len(sent)))

    for copy in meta_depth:
        copy.start()
    order = (0, 2, 1, 3)
    for d in (2, 1, 3):
        sent.append(send(0, d, depth[d], len(sent)))
    for copy in meta_depth:
        copy.wait_recv()
    for copy in meta_column:
        copy.start()
    for d in order:
        if d:
            arrived(d)
        for g in (3, 1, 2) if d in (0, 2) else (1, 2):
            sent.append(send(d, g * 4 + d, column[g], len(sent)))
        to_twin(d)
    for n in range(steps):
        gate_copy(n).start()
        up_copy(n).start()
    for copy in meta_column:
        copy.wait_recv()
    meta_twin.start()
    arrived(12)
    sent.append(send(12, 13, depth[1], len(sent)))
    to_twin(12)
    meta_twin.wait_recv()

    info = meta[...].astype(jnp.float32)[:, 0:8, :].reshape(total, META)
    lane = lax.broadcasted_iota(jnp.int32, (total, META), 1)
    mine = (lane % 32) == expert
    weight = jnp.sum(jnp.where(mine & (lane < 96), info, 0.0), axis=1, keepdims=True)
    slot = jnp.sum(jnp.where(mine & (lane >= 96), info, 0.0), axis=1, keepdims=True)
    place = lax.broadcasted_iota(jnp.int32, (total, total), 0)
    far_core = (core + place // 128) % 2
    far_x = (x + (place // 64) % 2) % 2
    far_y = (y + (place // 32) % 2) % 2
    far_z = ((z_high + (place // 16) % 2) % 2) * 2 + (z_low + (place // 8) % 2) % 2
    base = ((far_z * 2 + far_y) * 4 + far_x * 2 + far_core) * 8
    spot = lax.broadcasted_iota(jnp.int32, (total, total), 1) - base
    placing = (spot.astype(jnp.float32) == slot).astype(jnp.float32).T.astype(jnp.bfloat16)

    for copy in saved:
        copy.wait()
    for n in range(4):
        size = hidden // 4
        part = slice(n * size, (n + 1) * size)
        a = lax.dot_general(
            sgate_v[:, part], placing, LEADING, preferred_element_type=jnp.float32
        )
        b = lax.dot_general(sup_v[:, part], placing, LEADING, preferred_element_type=jnp.float32)
        q = jax.nn.sigmoid(a)
        up_f[part, :] = a * q
        gate_f[part, :] = b * q * (1.0 + a * (1.0 - q))
        for g in (1, 2):
            arrived(g * 4 + order[n])
            to_twin(g * 4 + order[n])
        if n == 0:
            arrived(14)
            sent.append(send(14, 15, depth[1], len(sent)))
            to_twin(14)
    for d in (1, 3):
        arrived(12 + d)
        to_twin(12 + d)

    quarter = half // 4
    for k in range(2):
        if k == 1:
            for index in range(16, 32):
                arrived(index)
        span = slice(k * 128, (k + 1) * 128)
        for n in range(4):
            part = blocks[k * 16 : k * 16 + 16, :, n * quarter : (n + 1) * quarter]
            part = part.astype(jnp.float32)
            for h in range(2):
                value = part[:, h * 8 : h * 8 + 8, :].reshape(128, quarter) * weight[span]
                start = h * half + n * quarter
                rows[start : start + quarter, span] = value.astype(jnp.bfloat16).T

    @pl.loop(0, hidden_steps)
    def _(n):
        down_copy(n).wait()
        part = pl.ds(pl.multiple_of(n * CHUNK, CHUNK), CHUNK)
        grad = jnp.dot(down_v[part, :], rows[...], preferred_element_type=jnp.float32)
        up_g[part, :] = (grad * up_f[part, :]).astype(jnp.bfloat16)
        gate_g[part, :] = (grad * gate_f[part, :]).astype(jnp.bfloat16)

    def a_copy(j):
        return pltpu.make_async_remote_copy(
            src_ref=a_send.at[j],
            dst_ref=a_recv.at[j],
            send_sem=as_sem.at[j],
            recv_sem=ar_sem.at[j],
            device_id=twin,
            device_id_type=MESH,
        )

    def b_copy(j, g):
        return pltpu.make_async_remote_copy(
            src_ref=b_send.at[j, g - 1],
            dst_ref=b_recv.at[j, g - 1],
            send_sem=bs_sem.at[j, g - 1],
            recv_sem=br_sem.at[j, g - 1],
            device_id=column[g],
            device_id_type=MESH,
        )

    def c_copy(j, d):
        return pltpu.make_async_remote_copy(
            src_ref=c_send.at[j, d - 1],
            dst_ref=c_recv.at[j, d - 1],
            send_sem=cs_sem.at[j, d - 1],
            recv_sem=cr_sem.at[j, d - 1],
            device_id=depth[d],
            device_id_type=MESH,
        )

    @pl.loop(0, steps + 3)
    def _(i):
        @pl.when(i < steps)
        def _():
            gate_copy(i).wait()
            up_copy(i).wait()
            part = pl.ds(pl.multiple_of(i * CHUNK, CHUNK), CHUNK)
            value = jnp.dot(
                gate_v[part, :], gate_g[...], preferred_element_type=jnp.float32
            ) + jnp.dot(up_v[part, :], up_g[...], preferred_element_type=jnp.float32)
            value = value.T
            a_send[i] = value[128:256].astype(jnp.bfloat16)
            own[i] = value[0:128]
            a_copy(i).start()

        @pl.when((i >= 1) & (i < steps + 1))
        def _():
            j = i - 1
            a_copy(j).wait_recv()
            value = own[j] + a_recv[j].astype(jnp.float32)
            for g in (3, 1, 2):
                b_send[j, g - 1] = value[g * 32 : g * 32 + 32].astype(jnp.bfloat16)
                b_copy(j, g).start()
            col[j] = value[0:32]

        @pl.when((i >= 2) & (i < steps + 2))
        def _():
            j = i - 2
            value = col[j]
            for g in (1, 2, 3):
                b_copy(j, g).wait_recv()
                value = value + b_recv[j, g - 1].astype(jnp.float32)
            for d in (2, 1, 3):
                line = value[d * 8 : d * 8 + 8]
                folded = jnp.concatenate([line[:, : CHUNK // 2], line[:, CHUNK // 2 :]], axis=0)
                c_send[j, d - 1] = folded.astype(jnp.bfloat16)
                c_copy(j, d).start()
            col[j, 0:8, :] = value[0:8]

        @pl.when(i >= 3)
        def _():
            j = i - 3
            value = col[j, 0:8, :]
            for d in (1, 2, 3):
                c_copy(j, d).wait_recv()
                folded = c_recv[j, d - 1].astype(jnp.float32)
                value = value + jnp.concatenate([folded[0:8], folded[8:16]], axis=1)
            part = pl.ds(pl.multiple_of(j * CHUNK, CHUNK), CHUNK)
            out[:, part] = value.astype(out.dtype)

    for copy in sent + meta_depth + meta_column + [meta_twin]:
        copy.wait_send()

    @pl.loop(0, steps)
    def _(j):
        a_copy(j).wait_send()
        for g in (1, 2, 3):
            b_copy(j, g).wait_send()
        for d in (1, 2, 3):
            c_copy(j, d).wait_send()


def fused_shards(out_grad, routes, gate_weight, gate_proj, up_proj, down_proj, saved_gate, saved_up):
    feature = out_grad.shape[1]
    hidden = gate_proj.shape[2]
    total = saved_gate.shape[1]
    steps = feature // CHUNK
    bf16, f32 = jnp.bfloat16, jnp.float32
    vmem = pl.BlockSpec(memory_space=pltpu.VMEM)
    anywhere = pl.BlockSpec(memory_space=pl.ANY)
    dma = pltpu.SemaphoreType.DMA
    flops = 2 * 3 * total * feature * hidden
    return pl.pallas_call(
        fused_kernel,
        out_shape=jax.ShapeDtypeStruct(out_grad.shape, bf16),
        in_specs=[vmem] * 3 + [anywhere] * 5,
        out_specs=vmem,
        scratch_shapes=[
            pltpu.VMEM((feature, hidden), bf16),
            pltpu.VMEM((feature, hidden), bf16),
            pltpu.VMEM((hidden, feature), bf16),
            pltpu.VMEM((total, hidden), bf16),
            pltpu.VMEM((total, hidden), bf16),
            pltpu.VMEM((32, 16, feature // 2), bf16),
            pltpu.VMEM((32, 16, META), bf16),
            pltpu.VMEM((feature, total), bf16),
            pltpu.VMEM((hidden, total), bf16),
            pltpu.VMEM((hidden, total), bf16),
            pltpu.VMEM((hidden, total), f32),
            pltpu.VMEM((hidden, total), f32),
            pltpu.VMEM((steps, 128, CHUNK), f32),
            pltpu.VMEM((steps, 128, CHUNK), bf16),
            pltpu.VMEM((steps, 128, CHUNK), bf16),
            pltpu.VMEM((steps, 32, CHUNK), f32),
            pltpu.VMEM((steps, 3, 32, CHUNK), bf16),
            pltpu.VMEM((steps, 3, 32, CHUNK), bf16),
            pltpu.VMEM((steps, 3, 16, CHUNK // 2), bf16),
            pltpu.VMEM((steps, 3, 16, CHUNK // 2), bf16),
            dma((3, max(steps, hidden // CHUNK))),
            dma((2,)),
            dma((7,)),
            dma((7,)),
            dma((31,)),
            dma((32,)),
            dma((steps,)),
            dma((steps,)),
            dma((steps, 3)),
            dma((steps, 3)),
            dma((steps, 3)),
            dma((steps, 3)),
        ],
        compiler_params=pltpu.CompilerParams(
            collective_id=0, has_side_effects=True, vmem_limit_bytes=60 * 1024 * 1024
        ),
        cost_estimate=pl.CostEstimate(
            flops=flops, bytes_accessed=3 * 2 * feature * hidden, transcendentals=total * hidden
        ),
    )(out_grad, routes.T, gate_weight.T, gate_proj, up_proj, down_proj, saved_gate, saved_up)


def rank_slots(flat_routes):
    count = flat_routes.shape[-1]
    positions = jnp.arange(count, dtype=jnp.int32)
    before = positions[:, None] < positions[None, :]
    matches = flat_routes[..., :, None] == flat_routes[..., None, :]
    return jnp.sum(jnp.logical_and(matches, before), axis=-2)


def expert_rows(grad_rows, gate_mat, up_mat, down_mat, pre_gate, pre_up):
    contract = (((1,), (1,)), ((), ()))
    hidden_grad = lax.dot_general(grad_rows, down_mat, contract, preferred_element_type=jnp.float32)
    gate_vals = pre_gate.astype(jnp.float32)
    up_vals = pre_up.astype(jnp.float32)
    sigmoid_gate = jax.nn.sigmoid(gate_vals)
    up_grad = (hidden_grad * gate_vals * sigmoid_gate).astype(jnp.bfloat16)
    gate_grad = (
        hidden_grad * up_vals * sigmoid_gate * (1.0 + gate_vals * (1.0 - sigmoid_gate))
    ).astype(jnp.bfloat16)
    partial_value = lax.dot_general(
        gate_grad, gate_mat, contract, preferred_element_type=jnp.float32
    )
    return partial_value + lax.dot_general(
        up_grad, up_mat, contract, preferred_element_type=jnp.float32
    )


def shards(out_grad, routes, gate_weight, gate_proj, up_proj, down_proj, saved_gate, saved_up):
    expert_count = lax.axis_size("expert")
    cut_count = lax.axis_size("cuts")
    tok_rows = out_grad.shape[0]
    feature_dim = out_grad.shape[1]
    slot_count = saved_gate.shape[1] // (expert_count * cut_count)
    flat_routes = routes.reshape(-1)
    slot_index = rank_slots(flat_routes[None, :])[0]
    own_spots = flat_routes * slot_count + slot_index
    routed = (gate_weight[:, :, None] * out_grad.astype(jnp.float32)[:, None, :]).astype(
        jnp.bfloat16
    )
    routed = routed.reshape(2 * tok_rows, feature_dim)
    places = jnp.arange(expert_count * slot_count, dtype=jnp.int32)
    placing = (places[:, None] == own_spots[None, :]).astype(jnp.bfloat16)
    outgoing = jnp.dot(placing, routed, preferred_element_type=jnp.float32).astype(jnp.bfloat16)
    outgoing = outgoing.reshape(expert_count, slot_count, feature_dim)
    arrived = lax.all_to_all(outgoing, "expert", split_axis=0, concat_axis=0, tiled=True)
    gathered = lax.all_gather(arrived, "cuts", axis=0, tiled=True).reshape(-1, feature_dim)
    gate_block = saved_gate[0]
    up_block = saved_up[0]
    own_rows = lax.psum_scatter(
        expert_rows(gathered, gate_proj[0], up_proj[0], down_proj[0], gate_block, up_block),
        "cuts",
        scatter_dimension=0,
        tiled=True,
    )
    own_rows = own_rows.reshape(expert_count, slot_count, feature_dim)
    returned = lax.all_to_all(own_rows, "expert", split_axis=0, concat_axis=0, tiled=True).reshape(
        -1, feature_dim
    )
    picked = returned[own_spots].reshape(tok_rows, 2, feature_dim)
    summed = jnp.sum(picked, axis=1)
    return summed.astype(jnp.bfloat16)


def solution(mesh):
    in_specs = (
        P(("expert", "cuts"), None),
        P(("expert", "cuts"), None),
        P(("expert", "cuts"), None),
        P("expert", None, "cuts"),
        P("expert", None, "cuts"),
        P("expert", "cuts", None),
        P("expert", None, "cuts"),
        P("expert", None, "cuts"),
    )
    out_specs = P(("expert", "cuts"), None)
    fused = (mesh.shape["expert"], mesh.shape["cuts"]) == (4, 8)
    body = fused_shards if fused else shards
    return jax.shard_map(body, mesh=mesh, in_specs=in_specs, out_specs=out_specs, check_vma=False)
```

```python
import jax
import jax.numpy as jnp
from jax import lax
from jax.experimental import pallas as pl
from jax.experimental.pallas import tpu as pltpu
from jax.sharding import PartitionSpec as P

MESH = pl.DeviceIdType.MESH
LEADING = (((0,), (0,)), ((), ()))
META = 128
CHUNK = 512


def upright(ref, choice):
    across = jnp.broadcast_to(ref[choice : choice + 1, :].astype(jnp.float32), (8, 8))
    keep = lax.broadcasted_iota(jnp.int32, (8, 8), 0) == lax.broadcasted_iota(jnp.int32, (8, 8), 1)
    return jnp.sum(jnp.where(keep, across, 0.0), axis=1, keepdims=True)


def fused_kernel(
    tok, routes, gates, gate_hbm, up_hbm, down_hbm, sgate_hbm, sup_hbm, out,
    gate_v, up_v, down_v, sgate_v, sup_v, blocks, meta, rows, gate_g, up_g, gate_f, up_f,
    own, a_send, a_recv, col, b_send, b_recv, c_send, c_recv,
    w_sem, s_sem, ms_sem, mr_sem, gs_sem, gr_sem, as_sem, ar_sem, bs_sem, br_sem, cs_sem, cr_sem,
):
    expert = lax.axis_index("expert")
    cut = lax.axis_index("cuts")
    x, core = expert // 2, expert % 2
    z, y = cut // 2, cut % 2
    feature = tok.shape[1]
    half = feature // 2
    hidden = down_v.shape[0]
    total = rows.shape[1]
    steps = feature // CHUNK
    hidden_steps = hidden // CHUNK

    column = [
        None,
        (expert, z * 2 + (1 - y)),
        ((1 - x) * 2 + core, cut),
        ((1 - x) * 2 + core, z * 2 + (1 - y)),
    ]
    z_high, z_low = z // 2, z % 2
    depth = [None] + [
        (expert, (((z_high + d // 2) % 2) * 2 + (z_low + d % 2) % 2) * 2 + y) for d in (1, 2, 3)
    ]
    twin = (x * 2 + (1 - core), cut)

    def down_copy(n):
        part = pl.ds(pl.multiple_of(n * CHUNK, CHUNK), CHUNK)
        return pltpu.make_async_copy(down_hbm.at[0, part], down_v.at[part], w_sem.at[0, n])

    def gate_copy(n):
        part = pl.ds(pl.multiple_of(n * CHUNK, CHUNK), CHUNK)
        return pltpu.make_async_copy(gate_hbm.at[0, part], gate_v.at[part], w_sem.at[1, n])

    def up_copy(n):
        part = pl.ds(pl.multiple_of(n * CHUNK, CHUNK), CHUNK)
        return pltpu.make_async_copy(up_hbm.at[0, part], up_v.at[part], w_sem.at[2, n])

    saved = [
        pltpu.make_async_copy(sgate_hbm.at[0], sgate_v, s_sem.at[0]),
        pltpu.make_async_copy(sup_hbm.at[0], sup_v, s_sem.at[1]),
    ]

    barrier = pltpu.get_barrier_semaphore()
    for peer in column[1:] + depth[1:] + [twin]:
        pl.semaphore_signal(barrier, inc=1, device_id=peer, device_id_type=MESH)

    for copy in saved:
        copy.start()
    for n in range(hidden_steps):
        down_copy(n).start()
    for n in range(steps):
        gate_copy(n).start()
        up_copy(n).start()

    lane = lax.broadcasted_iota(jnp.int32, (8, META), 1)
    level = lane // 32
    name = lane % 32
    first = (upright(routes, 0) == name.astype(jnp.float32)).astype(jnp.float32)
    second = (upright(routes, 1) == name.astype(jnp.float32)).astype(jnp.float32)
    hit = first + second
    weight = first * upright(gates, 0) + second * upright(gates, 1)
    sub = lax.broadcasted_iota(jnp.int32, (8, META), 0)
    slot = jnp.zeros((8, META), jnp.float32)
    for t in range(7):
        slot = slot + jnp.where(sub > t, hit[t : t + 1, :], 0.0)
    slot = jnp.where(hit > 0.0, slot, -1.0)
    high = weight.astype(jnp.bfloat16).astype(jnp.float32)
    middle = (weight - high).astype(jnp.bfloat16).astype(jnp.float32)
    low = weight - high - middle
    routing = jnp.where(
        level == 0, high, jnp.where(level == 1, middle, jnp.where(level == 2, low, slot))
    )
    meta[0] = jnp.concatenate([routing, jnp.zeros_like(routing)], axis=0).astype(jnp.bfloat16)
    tokens = tok[...].astype(jnp.float32)
    stacked = jnp.concatenate([tokens[:, :half], tokens[:, half:]], axis=0)
    blocks[0] = stacked.astype(jnp.bfloat16)

    pl.semaphore_wait(barrier, 7)

    def send(source, target, peer, sem):
        copy = pltpu.make_async_remote_copy(
            src_ref=blocks.at[source],
            dst_ref=blocks.at[target],
            send_sem=gs_sem.at[sem],
            recv_sem=gr_sem.at[target],
            device_id=peer,
            device_id_type=MESH,
        )
        copy.start()
        return copy

    def arrived(index):
        pltpu.make_async_remote_copy(
            src_ref=blocks.at[index],
            dst_ref=blocks.at[index],
            send_sem=gs_sem.at[0],
            recv_sem=gr_sem.at[index],
            device_id=twin,
            device_id_type=MESH,
        ).wait_recv()

    sent = []
    def meta_copy(n, source, target, count, peer):
        return pltpu.make_async_remote_copy(
            src_ref=meta.at[pl.ds(source, count)],
            dst_ref=meta.at[pl.ds(target, count)],
            send_sem=ms_sem.at[n],
            recv_sem=mr_sem.at[n],
            device_id=peer,
            device_id_type=MESH,
        )

    meta_depth = [meta_copy(d - 1, 0, d, 1, depth[d]) for d in (1, 2, 3)]
    meta_column = [meta_copy(2 + g, 0, g * 4, 4, column[g]) for g in (1, 2, 3)]
    meta_twin = meta_copy(6, 0, 16, 16, twin)

    def to_twin(index):
        sent.append(send(index, 16 + index, twin, len(sent)))

    for copy in meta_depth:
        copy.start()
    order = (0, 2, 1, 3)
    for d in (2, 1, 3):
        sent.append(send(0, d, depth[d], len(sent)))
    for copy in meta_depth:
        copy.wait_recv()
    for copy in meta_column:
        copy.start()
    for d in order:
        if d:
            arrived(d)
        for g in (3, 1, 2) if d in (0, 2) else (1, 2):
            sent.append(send(d, g * 4 + d, column[g], len(sent)))
        to_twin(d)
    for copy in meta_column:
        copy.wait_recv()
    meta_twin.start()
    arrived(12)
    sent.append(send(12, 13, depth[1], len(sent)))
    to_twin(12)
    meta_twin.wait_recv()

    info = meta[...].astype(jnp.float32)[:, 0:8, :].reshape(total, META)
    lane = lax.broadcasted_iota(jnp.int32, (total, META), 1)
    mine = (lane % 32) == expert
    weight = jnp.sum(jnp.where(mine & (lane < 96), info, 0.0), axis=1, keepdims=True)
    slot = jnp.sum(jnp.where(mine & (lane >= 96), info, 0.0), axis=1, keepdims=True)
    place = lax.broadcasted_iota(jnp.int32, (total, total), 0)
    far_core = (core + place // 128) % 2
    far_x = (x + (place // 64) % 2) % 2
    far_y = (y + (place // 32) % 2) % 2
    far_z = ((z_high + (place // 16) % 2) % 2) * 2 + (z_low + (place // 8) % 2) % 2
    base = ((far_z * 2 + far_y) * 4 + far_x * 2 + far_core) * 8
    spot = lax.broadcasted_iota(jnp.int32, (total, total), 1) - base
    placing = (spot.astype(jnp.float32) == slot).astype(jnp.float32).T.astype(jnp.bfloat16)

    for copy in saved:
        copy.wait()
    for n in range(4):
        size = hidden // 4
        part = slice(n * size, (n + 1) * size)
        a = lax.dot_general(
            sgate_v[:, part], placing, LEADING, preferred_element_type=jnp.float32
        )
        b = lax.dot_general(sup_v[:, part], placing, LEADING, preferred_element_type=jnp.float32)
        q = jax.nn.sigmoid(a)
        up_f[part, :] = a * q
        gate_f[part, :] = b * q * (1.0 + a * (1.0 - q))
        for g in (1, 2):
            arrived(g * 4 + order[n])
            to_twin(g * 4 + order[n])
        if n == 0:
            arrived(14)
            sent.append(send(14, 15, depth[1], len(sent)))
            to_twin(14)
    for d in (1, 3):
        arrived(12 + d)
        to_twin(12 + d)

    quarter = half // 4
    for k in range(2):
        if k == 1:
            for index in range(16, 32):
                arrived(index)
        span = slice(k * 128, (k + 1) * 128)
        for n in range(4):
            part = blocks[k * 16 : k * 16 + 16, :, n * quarter : (n + 1) * quarter]
            part = part.astype(jnp.float32)
            for h in range(2):
                value = part[:, h * 8 : h * 8 + 8, :].reshape(128, quarter) * weight[span]
                start = h * half + n * quarter
                rows[start : start + quarter, span] = value.astype(jnp.bfloat16).T

    @pl.loop(0, hidden_steps)
    def _(n):
        down_copy(n).wait()
        part = pl.ds(pl.multiple_of(n * CHUNK, CHUNK), CHUNK)
        grad = jnp.dot(down_v[part, :], rows[...], preferred_element_type=jnp.float32)
        up_g[part, :] = (grad * up_f[part, :]).astype(jnp.bfloat16)
        gate_g[part, :] = (grad * gate_f[part, :]).astype(jnp.bfloat16)

    def a_copy(j):
        return pltpu.make_async_remote_copy(
            src_ref=a_send.at[j],
            dst_ref=a_recv.at[j],
            send_sem=as_sem.at[j],
            recv_sem=ar_sem.at[j],
            device_id=twin,
            device_id_type=MESH,
        )

    def b_copy(j, g):
        return pltpu.make_async_remote_copy(
            src_ref=b_send.at[j, g - 1],
            dst_ref=b_recv.at[j, g - 1],
            send_sem=bs_sem.at[j, g - 1],
            recv_sem=br_sem.at[j, g - 1],
            device_id=column[g],
            device_id_type=MESH,
        )

    def c_copy(j, d):
        return pltpu.make_async_remote_copy(
            src_ref=c_send.at[j, d - 1],
            dst_ref=c_recv.at[j, d - 1],
            send_sem=cs_sem.at[j, d - 1],
            recv_sem=cr_sem.at[j, d - 1],
            device_id=depth[d],
            device_id_type=MESH,
        )

    @pl.loop(0, steps + 5)
    def _(i):
        @pl.when(i < steps)
        def _():
            gate_copy(i).wait()
            up_copy(i).wait()
            part = pl.ds(pl.multiple_of(i * CHUNK, CHUNK), CHUNK)
            value = jnp.dot(
                gate_v[part, :], gate_g[...], preferred_element_type=jnp.float32
            ) + jnp.dot(up_v[part, :], up_g[...], preferred_element_type=jnp.float32)
            value = value.T
            a_send[i] = value[128:256].astype(jnp.bfloat16)
            own[i] = value[0:128]
            a_copy(i).start()

        @pl.when((i >= 1) & (i < steps + 1))
        def _():
            j = i - 1
            a_copy(j).wait_recv()
            value = own[j] + a_recv[j].astype(jnp.float32)
            for g in (3, 1, 2):
                b_send[j, g - 1] = value[g * 32 : g * 32 + 32].astype(jnp.bfloat16)
                b_copy(j, g).start()
            col[j] = value[0:32]

        @pl.when((i >= 3) & (i < steps + 3))
        def _():
            j = i - 3
            value = col[j]
            for g in (1, 2, 3):
                b_copy(j, g).wait_recv()
                value = value + b_recv[j, g - 1].astype(jnp.float32)
            for d in (2, 1, 3):
                line = value[d * 8 : d * 8 + 8]
                folded = jnp.concatenate([line[:, : CHUNK // 2], line[:, CHUNK // 2 :]], axis=0)
                c_send[j, d - 1] = folded.astype(jnp.bfloat16)
                c_copy(j, d).start()
            col[j, 0:8, :] = value[0:8]

        @pl.when(i >= 5)
        def _():
            j = i - 5
            value = col[j, 0:8, :]
            for d in (1, 2, 3):
                c_copy(j, d).wait_recv()
                folded = c_recv[j, d - 1].astype(jnp.float32)
                value = value + jnp.concatenate([folded[0:8], folded[8:16]], axis=1)
            part = pl.ds(pl.multiple_of(j * CHUNK, CHUNK), CHUNK)
            out[:, part] = value.astype(out.dtype)

    for copy in sent + meta_depth + meta_column + [meta_twin]:
        copy.wait_send()

    @pl.loop(0, steps)
    def _(j):
        a_copy(j).wait_send()
        for g in (1, 2, 3):
            b_copy(j, g).wait_send()
        for d in (1, 2, 3):
            c_copy(j, d).wait_send()


def fused_shards(out_grad, routes, gate_weight, gate_proj, up_proj, down_proj, saved_gate, saved_up):
    feature = out_grad.shape[1]
    hidden = gate_proj.shape[2]
    total = saved_gate.shape[1]
    steps = feature // CHUNK
    bf16, f32 = jnp.bfloat16, jnp.float32
    vmem = pl.BlockSpec(memory_space=pltpu.VMEM)
    anywhere = pl.BlockSpec(memory_space=pl.ANY)
    dma = pltpu.SemaphoreType.DMA
    flops = 2 * 3 * total * feature * hidden
    return pl.pallas_call(
        fused_kernel,
        out_shape=jax.ShapeDtypeStruct(out_grad.shape, bf16),
        in_specs=[vmem] * 3 + [anywhere] * 5,
        out_specs=vmem,
        scratch_shapes=[
            pltpu.VMEM((feature, hidden), bf16),
            pltpu.VMEM((feature, hidden), bf16),
            pltpu.VMEM((hidden, feature), bf16),
            pltpu.VMEM((total, hidden), bf16),
            pltpu.VMEM((total, hidden), bf16),
            pltpu.VMEM((32, 16, feature // 2), bf16),
            pltpu.VMEM((32, 16, META), bf16),
            pltpu.VMEM((feature, total), bf16),
            pltpu.VMEM((hidden, total), bf16),
            pltpu.VMEM((hidden, total), bf16),
            pltpu.VMEM((hidden, total), f32),
            pltpu.VMEM((hidden, total), f32),
            pltpu.VMEM((steps, 128, CHUNK), f32),
            pltpu.VMEM((steps, 128, CHUNK), bf16),
            pltpu.VMEM((steps, 128, CHUNK), bf16),
            pltpu.VMEM((steps, 32, CHUNK), f32),
            pltpu.VMEM((steps, 3, 32, CHUNK), bf16),
            pltpu.VMEM((steps, 3, 32, CHUNK), bf16),
            pltpu.VMEM((steps, 3, 16, CHUNK // 2), bf16),
            pltpu.VMEM((steps, 3, 16, CHUNK // 2), bf16),
            dma((3, max(steps, hidden // CHUNK))),
            dma((2,)),
            dma((7,)),
            dma((7,)),
            dma((31,)),
            dma((32,)),
            dma((steps,)),
            dma((steps,)),
            dma((steps, 3)),
            dma((steps, 3)),
            dma((steps, 3)),
            dma((steps, 3)),
        ],
        compiler_params=pltpu.CompilerParams(
            collective_id=0, has_side_effects=True, vmem_limit_bytes=60 * 1024 * 1024
        ),
        cost_estimate=pl.CostEstimate(
            flops=flops, bytes_accessed=3 * 2 * feature * hidden, transcendentals=total * hidden
        ),
    )(out_grad, routes.T, gate_weight.T, gate_proj, up_proj, down_proj, saved_gate, saved_up)


def rank_slots(flat_routes):
    count = flat_routes.shape[-1]
    positions = jnp.arange(count, dtype=jnp.int32)
    before = positions[:, None] < positions[None, :]
    matches = flat_routes[..., :, None] == flat_routes[..., None, :]
    return jnp.sum(jnp.logical_and(matches, before), axis=-2)


def expert_rows(grad_rows, gate_mat, up_mat, down_mat, pre_gate, pre_up):
    contract = (((1,), (1,)), ((), ()))
    hidden_grad = lax.dot_general(grad_rows, down_mat, contract, preferred_element_type=jnp.float32)
    gate_vals = pre_gate.astype(jnp.float32)
    up_vals = pre_up.astype(jnp.float32)
    sigmoid_gate = jax.nn.sigmoid(gate_vals)
    up_grad = (hidden_grad * gate_vals * sigmoid_gate).astype(jnp.bfloat16)
    gate_grad = (
        hidden_grad * up_vals * sigmoid_gate * (1.0 + gate_vals * (1.0 - sigmoid_gate))
    ).astype(jnp.bfloat16)
    partial_value = lax.dot_general(
        gate_grad, gate_mat, contract, preferred_element_type=jnp.float32
    )
    return partial_value + lax.dot_general(
        up_grad, up_mat, contract, preferred_element_type=jnp.float32
    )


def shards(out_grad, routes, gate_weight, gate_proj, up_proj, down_proj, saved_gate, saved_up):
    expert_count = lax.axis_size("expert")
    cut_count = lax.axis_size("cuts")
    tok_rows = out_grad.shape[0]
    feature_dim = out_grad.shape[1]
    slot_count = saved_gate.shape[1] // (expert_count * cut_count)
    flat_routes = routes.reshape(-1)
    slot_index = rank_slots(flat_routes[None, :])[0]
    own_spots = flat_routes * slot_count + slot_index
    routed = (gate_weight[:, :, None] * out_grad.astype(jnp.float32)[:, None, :]).astype(
        jnp.bfloat16
    )
    routed = routed.reshape(2 * tok_rows, feature_dim)
    places = jnp.arange(expert_count * slot_count, dtype=jnp.int32)
    placing = (places[:, None] == own_spots[None, :]).astype(jnp.bfloat16)
    outgoing = jnp.dot(placing, routed, preferred_element_type=jnp.float32).astype(jnp.bfloat16)
    outgoing = outgoing.reshape(expert_count, slot_count, feature_dim)
    arrived = lax.all_to_all(outgoing, "expert", split_axis=0, concat_axis=0, tiled=True)
    gathered = lax.all_gather(arrived, "cuts", axis=0, tiled=True).reshape(-1, feature_dim)
    gate_block = saved_gate[0]
    up_block = saved_up[0]
    own_rows = lax.psum_scatter(
        expert_rows(gathered, gate_proj[0], up_proj[0], down_proj[0], gate_block, up_block),
        "cuts",
        scatter_dimension=0,
        tiled=True,
    )
    own_rows = own_rows.reshape(expert_count, slot_count, feature_dim)
    returned = lax.all_to_all(own_rows, "expert", split_axis=0, concat_axis=0, tiled=True).reshape(
        -1, feature_dim
    )
    picked = returned[own_spots].reshape(tok_rows, 2, feature_dim)
    summed = jnp.sum(picked, axis=1)
    return summed.astype(jnp.bfloat16)


def solution(mesh):
    in_specs = (
        P(("expert", "cuts"), None),
        P(("expert", "cuts"), None),
        P(("expert", "cuts"), None),
        P("expert", None, "cuts"),
        P("expert", None, "cuts"),
        P("expert", "cuts", None),
        P("expert", None, "cuts"),
        P("expert", None, "cuts"),
    )
    out_specs = P(("expert", "cuts"), None)
    fused = (mesh.shape["expert"], mesh.shape["cuts"]) == (4, 8)
    body = fused_shards if fused else shards
    return jax.shard_map(body, mesh=mesh, in_specs=in_specs, out_specs=out_specs, check_vma=False)
```

```python
import jax
import jax.numpy as jnp
from jax import lax
from jax.experimental import pallas as pl
from jax.experimental.pallas import tpu as pltpu
from jax.sharding import PartitionSpec as P

MESH = pl.DeviceIdType.MESH
LEADING = (((0,), (0,)), ((), ()))
META = 128
CHUNK = 512


def upright(ref, choice):
    across = jnp.broadcast_to(ref[choice : choice + 1, :].astype(jnp.float32), (8, 8))
    keep = lax.broadcasted_iota(jnp.int32, (8, 8), 0) == lax.broadcasted_iota(jnp.int32, (8, 8), 1)
    return jnp.sum(jnp.where(keep, across, 0.0), axis=1, keepdims=True)


def fused_kernel(
    tok, routes, gates, gate_hbm, up_hbm, down_hbm, sgate_hbm, sup_hbm, out,
    gate_v, up_v, down_v, sgate_v, sup_v, blocks, meta, rows, gate_g, up_g, gate_f, up_f,
    own, a_send, a_recv, col, b_send, b_recv, c_send, c_recv,
    w_sem, s_sem, ms_sem, mr_sem, gs_sem, gr_sem, as_sem, ar_sem, bs_sem, br_sem, cs_sem, cr_sem,
):
    expert = lax.axis_index("expert")
    cut = lax.axis_index("cuts")
    x, core = expert // 2, expert % 2
    z, y = cut // 2, cut % 2
    feature = tok.shape[1]
    half = feature // 2
    hidden = down_v.shape[0]
    total = rows.shape[1]
    steps = feature // CHUNK
    hidden_steps = hidden // CHUNK

    column = [
        None,
        (expert, z * 2 + (1 - y)),
        ((1 - x) * 2 + core, cut),
        ((1 - x) * 2 + core, z * 2 + (1 - y)),
    ]
    z_high, z_low = z // 2, z % 2
    depth = [None] + [
        (expert, (((z_high + d // 2) % 2) * 2 + (z_low + d % 2) % 2) * 2 + y) for d in (1, 2, 3)
    ]
    twin = (x * 2 + (1 - core), cut)

    def down_copy(n):
        part = pl.ds(pl.multiple_of(n * CHUNK, CHUNK), CHUNK)
        return pltpu.make_async_copy(down_hbm.at[0, part], down_v.at[part], w_sem.at[0, n])

    def gate_copy(n):
        part = pl.ds(pl.multiple_of(n * CHUNK, CHUNK), CHUNK)
        return pltpu.make_async_copy(gate_hbm.at[0, part], gate_v.at[part], w_sem.at[1, n])

    def up_copy(n):
        part = pl.ds(pl.multiple_of(n * CHUNK, CHUNK), CHUNK)
        return pltpu.make_async_copy(up_hbm.at[0, part], up_v.at[part], w_sem.at[2, n])

    saved = [
        pltpu.make_async_copy(sgate_hbm.at[0], sgate_v, s_sem.at[0]),
        pltpu.make_async_copy(sup_hbm.at[0], sup_v, s_sem.at[1]),
    ]

    barrier = pltpu.get_barrier_semaphore()
    for peer in column[1:] + depth[1:] + [twin]:
        pl.semaphore_signal(barrier, inc=1, device_id=peer, device_id_type=MESH)

    for copy in saved:
        copy.start()
    for n in range(hidden_steps):
        down_copy(n).start()
    for n in range(steps):
        gate_copy(n).start()
        up_copy(n).start()

    lane = lax.broadcasted_iota(jnp.int32, (8, META), 1)
    level = lane // 32
    name = lane % 32
    first = (upright(routes, 0) == name.astype(jnp.float32)).astype(jnp.float32)
    second = (upright(routes, 1) == name.astype(jnp.float32)).astype(jnp.float32)
    hit = first + second
    weight = first * upright(gates, 0) + second * upright(gates, 1)
    sub = lax.broadcasted_iota(jnp.int32, (8, META), 0)
    slot = jnp.zeros((8, META), jnp.float32)
    for t in range(7):
        slot = slot + jnp.where(sub > t, hit[t : t + 1, :], 0.0)
    slot = jnp.where(hit > 0.0, slot, -1.0)
    high = weight.astype(jnp.bfloat16).astype(jnp.float32)
    middle = (weight - high).astype(jnp.bfloat16).astype(jnp.float32)
    low = weight - high - middle
    routing = jnp.where(
        level == 0, high, jnp.where(level == 1, middle, jnp.where(level == 2, low, slot))
    )
    meta[0] = jnp.concatenate([routing, jnp.zeros_like(routing)], axis=0).astype(jnp.bfloat16)
    tokens = tok[...].astype(jnp.float32)
    stacked = jnp.concatenate([tokens[:, :half], tokens[:, half:]], axis=0)
    blocks[0] = stacked.astype(jnp.bfloat16)

    pl.semaphore_wait(barrier, 7)

    def send(source, target, peer, sem):
        copy = pltpu.make_async_remote_copy(
            src_ref=blocks.at[source],
            dst_ref=blocks.at[target],
            send_sem=gs_sem.at[sem],
            recv_sem=gr_sem.at[target],
            device_id=peer,
            device_id_type=MESH,
        )
        copy.start()
        return copy

    def arrived(index):
        pltpu.make_async_remote_copy(
            src_ref=blocks.at[index],
            dst_ref=blocks.at[index],
            send_sem=gs_sem.at[0],
            recv_sem=gr_sem.at[index],
            device_id=twin,
            device_id_type=MESH,
        ).wait_recv()

    sent = []
    def meta_copy(n, source, target, count, peer):
        return pltpu.make_async_remote_copy(
            src_ref=meta.at[pl.ds(source, count)],
            dst_ref=meta.at[pl.ds(target, count)],
            send_sem=ms_sem.at[n],
            recv_sem=mr_sem.at[n],
            device_id=peer,
            device_id_type=MESH,
        )

    meta_depth = [meta_copy(d - 1, 0, d, 1, depth[d]) for d in (1, 2, 3)]
    meta_column = [meta_copy(2 + g, 0, g * 4, 4, column[g]) for g in (1, 2, 3)]
    meta_twin = meta_copy(6, 0, 16, 16, twin)

    def to_twin(index):
        sent.append(send(index, 16 + index, twin, len(sent)))

    for copy in meta_depth:
        copy.start()
    order = (0, 2, 1, 3)
    for d in (2, 1, 3):
        sent.append(send(0, d, depth[d], len(sent)))
    for copy in meta_depth:
        copy.wait_recv()
    for copy in meta_column:
        copy.start()
    for d in order:
        if d:
            arrived(d)
        for g in (3, 1, 2) if d in (0, 2) else (1, 2):
            sent.append(send(d, g * 4 + d, column[g], len(sent)))
        to_twin(d)
    for copy in meta_column:
        copy.wait_recv()
    meta_twin.start()
    arrived(12)
    sent.append(send(12, 13, depth[1], len(sent)))
    to_twin(12)
    meta_twin.wait_recv()

    info = meta[...].astype(jnp.float32)[:, 0:8, :].reshape(total, META)
    lane = lax.broadcasted_iota(jnp.int32, (total, META), 1)
    mine = (lane % 32) == expert
    weight = jnp.sum(jnp.where(mine & (lane < 96), info, 0.0), axis=1, keepdims=True)
    slot = jnp.sum(jnp.where(mine & (lane >= 96), info, 0.0), axis=1, keepdims=True)
    place = lax.broadcasted_iota(jnp.int32, (total, total), 0)
    far_core = (core + place // 128) % 2
    far_x = (x + (place // 64) % 2) % 2
    far_y = (y + (place // 32) % 2) % 2
    far_z = ((z_high + (place // 16) % 2) % 2) * 2 + (z_low + (place // 8) % 2) % 2
    base = ((far_z * 2 + far_y) * 4 + far_x * 2 + far_core) * 8
    spot = lax.broadcasted_iota(jnp.int32, (total, total), 1) - base
    placing = (spot.astype(jnp.float32) == slot).astype(jnp.float32).T.astype(jnp.bfloat16)

    for copy in saved:
        copy.wait()
    for n in range(4):
        size = hidden // 4
        part = slice(n * size, (n + 1) * size)
        a = lax.dot_general(
            sgate_v[:, part], placing, LEADING, preferred_element_type=jnp.float32
        )
        b = lax.dot_general(sup_v[:, part], placing, LEADING, preferred_element_type=jnp.float32)
        q = jax.nn.sigmoid(a)
        up_f[part, :] = a * q
        gate_f[part, :] = b * q * (1.0 + a * (1.0 - q))
        for g in (1, 2):
            arrived(g * 4 + order[n])
            to_twin(g * 4 + order[n])
        if n == 0:
            arrived(14)
            sent.append(send(14, 15, depth[1], len(sent)))
            to_twin(14)
    for d in (1, 3):
        arrived(12 + d)
        to_twin(12 + d)

    quarter = half // 4
    for k in range(2):
        if k == 1:
            for index in range(16, 32):
                arrived(index)
        span = slice(k * 128, (k + 1) * 128)
        for n in range(4):
            part = blocks[k * 16 : k * 16 + 16, :, n * quarter : (n + 1) * quarter]
            part = part.astype(jnp.float32)
            for h in range(2):
                value = part[:, h * 8 : h * 8 + 8, :].reshape(128, quarter) * weight[span]
                start = h * half + n * quarter
                rows[start : start + quarter, span] = value.astype(jnp.bfloat16).T

    @pl.loop(0, hidden_steps)
    def _(n):
        down_copy(n).wait()
        part = pl.ds(pl.multiple_of(n * CHUNK, CHUNK), CHUNK)
        grad = jnp.dot(down_v[part, :], rows[...], preferred_element_type=jnp.float32)
        up_g[part, :] = (grad * up_f[part, :]).astype(jnp.bfloat16)
        gate_g[part, :] = (grad * gate_f[part, :]).astype(jnp.bfloat16)

    def a_copy(j):
        return pltpu.make_async_remote_copy(
            src_ref=a_send.at[j],
            dst_ref=a_recv.at[j],
            send_sem=as_sem.at[j],
            recv_sem=ar_sem.at[j],
            device_id=twin,
            device_id_type=MESH,
        )

    def b_copy(j, g):
        return pltpu.make_async_remote_copy(
            src_ref=b_send.at[j, g - 1],
            dst_ref=b_recv.at[j, g - 1],
            send_sem=bs_sem.at[j, g - 1],
            recv_sem=br_sem.at[j, g - 1],
            device_id=column[g],
            device_id_type=MESH,
        )

    def c_copy(j, d):
        return pltpu.make_async_remote_copy(
            src_ref=c_send.at[j, d - 1],
            dst_ref=c_recv.at[j, d - 1],
            send_sem=cs_sem.at[j, d - 1],
            recv_sem=cr_sem.at[j, d - 1],
            device_id=depth[d],
            device_id_type=MESH,
        )

    @pl.loop(0, steps + 5)
    def _(i):
        @pl.when(i < steps)
        def _():
            gate_copy(i).wait()
            up_copy(i).wait()
            part = pl.ds(pl.multiple_of(i * CHUNK, CHUNK), CHUNK)
            value = jnp.dot(
                gate_v[part, :], gate_g[...], preferred_element_type=jnp.float32
            ) + jnp.dot(up_v[part, :], up_g[...], preferred_element_type=jnp.float32)
            a_send[i] = value[:, 128:256].astype(jnp.bfloat16)
            a_copy(i).start()
            own[i] = value[:, 0:128]

        @pl.when((i >= 1) & (i < steps + 1))
        def _():
            j = i - 1
            a_copy(j).wait_recv()
            value = (own[j] + a_recv[j].astype(jnp.float32)).T
            for g in (3, 1, 2):
                b_send[j, g - 1] = value[g * 32 : g * 32 + 32].astype(jnp.bfloat16)
                b_copy(j, g).start()
            col[j] = value[0:32]

        @pl.when((i >= 3) & (i < steps + 3))
        def _():
            j = i - 3
            value = col[j]
            for g in (1, 2, 3):
                b_copy(j, g).wait_recv()
                value = value + b_recv[j, g - 1].astype(jnp.float32)
            for d in (2, 1, 3):
                line = value[d * 8 : d * 8 + 8]
                folded = jnp.concatenate([line[:, : CHUNK // 2], line[:, CHUNK // 2 :]], axis=0)
                c_send[j, d - 1] = folded.astype(jnp.bfloat16)
                c_copy(j, d).start()
            col[j, 0:8, :] = value[0:8]

        @pl.when(i >= 5)
        def _():
            j = i - 5
            value = col[j, 0:8, :]
            for d in (1, 2, 3):
                c_copy(j, d).wait_recv()
                folded = c_recv[j, d - 1].astype(jnp.float32)
                value = value + jnp.concatenate([folded[0:8], folded[8:16]], axis=1)
            part = pl.ds(pl.multiple_of(j * CHUNK, CHUNK), CHUNK)
            out[:, part] = value.astype(out.dtype)

    for copy in sent + meta_depth + meta_column + [meta_twin]:
        copy.wait_send()

    @pl.loop(0, steps)
    def _(j):
        a_copy(j).wait_send()
        for g in (1, 2, 3):
            b_copy(j, g).wait_send()
        for d in (1, 2, 3):
            c_copy(j, d).wait_send()


def fused_shards(out_grad, routes, gate_weight, gate_proj, up_proj, down_proj, saved_gate, saved_up):
    feature = out_grad.shape[1]
    hidden = gate_proj.shape[2]
    total = saved_gate.shape[1]
    steps = feature // CHUNK
    bf16, f32 = jnp.bfloat16, jnp.float32
    vmem = pl.BlockSpec(memory_space=pltpu.VMEM)
    anywhere = pl.BlockSpec(memory_space=pl.ANY)
    dma = pltpu.SemaphoreType.DMA
    flops = 2 * 3 * total * feature * hidden
    return pl.pallas_call(
        fused_kernel,
        out_shape=jax.ShapeDtypeStruct(out_grad.shape, bf16),
        in_specs=[vmem] * 3 + [anywhere] * 5,
        out_specs=vmem,
        scratch_shapes=[
            pltpu.VMEM((feature, hidden), bf16),
            pltpu.VMEM((feature, hidden), bf16),
            pltpu.VMEM((hidden, feature), bf16),
            pltpu.VMEM((total, hidden), bf16),
            pltpu.VMEM((total, hidden), bf16),
            pltpu.VMEM((32, 16, feature // 2), bf16),
            pltpu.VMEM((32, 16, META), bf16),
            pltpu.VMEM((feature, total), bf16),
            pltpu.VMEM((hidden, total), bf16),
            pltpu.VMEM((hidden, total), bf16),
            pltpu.VMEM((hidden, total), f32),
            pltpu.VMEM((hidden, total), f32),
            pltpu.VMEM((steps, CHUNK, 128), f32),
            pltpu.VMEM((steps, CHUNK, 128), bf16),
            pltpu.VMEM((steps, CHUNK, 128), bf16),
            pltpu.VMEM((steps, 32, CHUNK), f32),
            pltpu.VMEM((steps, 3, 32, CHUNK), bf16),
            pltpu.VMEM((steps, 3, 32, CHUNK), bf16),
            pltpu.VMEM((steps, 3, 16, CHUNK // 2), bf16),
            pltpu.VMEM((steps, 3, 16, CHUNK // 2), bf16),
            dma((3, max(steps, hidden // CHUNK))),
            dma((2,)),
            dma((7,)),
            dma((7,)),
            dma((31,)),
            dma((32,)),
            dma((steps,)),
            dma((steps,)),
            dma((steps, 3)),
            dma((steps, 3)),
            dma((steps, 3)),
            dma((steps, 3)),
        ],
        compiler_params=pltpu.CompilerParams(
            collective_id=0, has_side_effects=True, vmem_limit_bytes=60 * 1024 * 1024
        ),
        cost_estimate=pl.CostEstimate(
            flops=flops, bytes_accessed=3 * 2 * feature * hidden, transcendentals=total * hidden
        ),
    )(out_grad, routes.T, gate_weight.T, gate_proj, up_proj, down_proj, saved_gate, saved_up)


def rank_slots(flat_routes):
    count = flat_routes.shape[-1]
    positions = jnp.arange(count, dtype=jnp.int32)
    before = positions[:, None] < positions[None, :]
    matches = flat_routes[..., :, None] == flat_routes[..., None, :]
    return jnp.sum(jnp.logical_and(matches, before), axis=-2)


def expert_rows(grad_rows, gate_mat, up_mat, down_mat, pre_gate, pre_up):
    contract = (((1,), (1,)), ((), ()))
    hidden_grad = lax.dot_general(grad_rows, down_mat, contract, preferred_element_type=jnp.float32)
    gate_vals = pre_gate.astype(jnp.float32)
    up_vals = pre_up.astype(jnp.float32)
    sigmoid_gate = jax.nn.sigmoid(gate_vals)
    up_grad = (hidden_grad * gate_vals * sigmoid_gate).astype(jnp.bfloat16)
    gate_grad = (
        hidden_grad * up_vals * sigmoid_gate * (1.0 + gate_vals * (1.0 - sigmoid_gate))
    ).astype(jnp.bfloat16)
    partial_value = lax.dot_general(
        gate_grad, gate_mat, contract, preferred_element_type=jnp.float32
    )
    return partial_value + lax.dot_general(
        up_grad, up_mat, contract, preferred_element_type=jnp.float32
    )


def shards(out_grad, routes, gate_weight, gate_proj, up_proj, down_proj, saved_gate, saved_up):
    expert_count = lax.axis_size("expert")
    cut_count = lax.axis_size("cuts")
    tok_rows = out_grad.shape[0]
    feature_dim = out_grad.shape[1]
    slot_count = saved_gate.shape[1] // (expert_count * cut_count)
    flat_routes = routes.reshape(-1)
    slot_index = rank_slots(flat_routes[None, :])[0]
    own_spots = flat_routes * slot_count + slot_index
    routed = (gate_weight[:, :, None] * out_grad.astype(jnp.float32)[:, None, :]).astype(
        jnp.bfloat16
    )
    routed = routed.reshape(2 * tok_rows, feature_dim)
    places = jnp.arange(expert_count * slot_count, dtype=jnp.int32)
    placing = (places[:, None] == own_spots[None, :]).astype(jnp.bfloat16)
    outgoing = jnp.dot(placing, routed, preferred_element_type=jnp.float32).astype(jnp.bfloat16)
    outgoing = outgoing.reshape(expert_count, slot_count, feature_dim)
    arrived = lax.all_to_all(outgoing, "expert", split_axis=0, concat_axis=0, tiled=True)
    gathered = lax.all_gather(arrived, "cuts", axis=0, tiled=True).reshape(-1, feature_dim)
    gate_block = saved_gate[0]
    up_block = saved_up[0]
    own_rows = lax.psum_scatter(
        expert_rows(gathered, gate_proj[0], up_proj[0], down_proj[0], gate_block, up_block),
        "cuts",
        scatter_dimension=0,
        tiled=True,
    )
    own_rows = own_rows.reshape(expert_count, slot_count, feature_dim)
    returned = lax.all_to_all(own_rows, "expert", split_axis=0, concat_axis=0, tiled=True).reshape(
        -1, feature_dim
    )
    picked = returned[own_spots].reshape(tok_rows, 2, feature_dim)
    summed = jnp.sum(picked, axis=1)
    return summed.astype(jnp.bfloat16)


def solution(mesh):
    in_specs = (
        P(("expert", "cuts"), None),
        P(("expert", "cuts"), None),
        P(("expert", "cuts"), None),
        P("expert", None, "cuts"),
        P("expert", None, "cuts"),
        P("expert", "cuts", None),
        P("expert", None, "cuts"),
        P("expert", None, "cuts"),
    )
    out_specs = P(("expert", "cuts"), None)
    fused = (mesh.shape["expert"], mesh.shape["cuts"]) == (4, 8)
    body = fused_shards if fused else shards
    return jax.shard_map(body, mesh=mesh, in_specs=in_specs, out_specs=out_specs, check_vma=False)
```

```python
import jax
import jax.numpy as jnp
from jax import lax
from jax.experimental import pallas as pl
from jax.experimental.pallas import tpu as pltpu
from jax.sharding import PartitionSpec as P

MESH = pl.DeviceIdType.MESH
LEADING = (((0,), (0,)), ((), ()))
META = 128
CHUNK = 512


def upright(ref, choice):
    across = jnp.broadcast_to(ref[choice : choice + 1, :].astype(jnp.float32), (8, 8))
    keep = lax.broadcasted_iota(jnp.int32, (8, 8), 0) == lax.broadcasted_iota(jnp.int32, (8, 8), 1)
    return jnp.sum(jnp.where(keep, across, 0.0), axis=1, keepdims=True)


def fused_kernel(
    tok, routes, gates, gate_hbm, up_hbm, down_hbm, sgate_hbm, sup_hbm, out,
    gate_v, up_v, down_v, sgate_v, sup_v, blocks, meta, rows, gate_g, up_g, gate_f, up_f,
    own, a_send, a_recv, col, b_send, b_recv, c_send, c_recv,
    w_sem, s_sem, ms_sem, mr_sem, gs_sem, gr_sem, as_sem, ar_sem, bs_sem, br_sem, cs_sem, cr_sem,
):
    expert = lax.axis_index("expert")
    cut = lax.axis_index("cuts")
    x, core = expert // 2, expert % 2
    z, y = cut // 2, cut % 2
    feature = tok.shape[1]
    half = feature // 2
    hidden = down_v.shape[0]
    total = rows.shape[1]
    steps = feature // CHUNK
    hidden_steps = hidden // CHUNK

    column = [
        None,
        (expert, z * 2 + (1 - y)),
        ((1 - x) * 2 + core, cut),
        ((1 - x) * 2 + core, z * 2 + (1 - y)),
    ]
    z_high, z_low = z // 2, z % 2
    depth = [None] + [
        (expert, (((z_high + d // 2) % 2) * 2 + (z_low + d % 2) % 2) * 2 + y) for d in (1, 2, 3)
    ]
    twin = (x * 2 + (1 - core), cut)

    def down_copy(n):
        part = pl.ds(pl.multiple_of(n * CHUNK, CHUNK), CHUNK)
        return pltpu.make_async_copy(down_hbm.at[0, part], down_v.at[part], w_sem.at[0, n])

    def gate_copy(n):
        part = pl.ds(pl.multiple_of(n * CHUNK, CHUNK), CHUNK)
        return pltpu.make_async_copy(gate_hbm.at[0, part], gate_v.at[part], w_sem.at[1, n])

    def up_copy(n):
        part = pl.ds(pl.multiple_of(n * CHUNK, CHUNK), CHUNK)
        return pltpu.make_async_copy(up_hbm.at[0, part], up_v.at[part], w_sem.at[2, n])

    saved = [
        pltpu.make_async_copy(sgate_hbm.at[0], sgate_v, s_sem.at[0]),
        pltpu.make_async_copy(sup_hbm.at[0], sup_v, s_sem.at[1]),
    ]

    barrier = pltpu.get_barrier_semaphore()
    for peer in column[1:] + depth[1:] + [twin]:
        pl.semaphore_signal(barrier, inc=1, device_id=peer, device_id_type=MESH)

    for copy in saved:
        copy.start()
    for n in range(hidden_steps):
        down_copy(n).start()
    for n in range(steps):
        gate_copy(n).start()
        up_copy(n).start()

    lane = lax.broadcasted_iota(jnp.int32, (8, META), 1)
    level = lane // 32
    name = lane % 32
    first = (upright(routes, 0) == name.astype(jnp.float32)).astype(jnp.float32)
    second = (upright(routes, 1) == name.astype(jnp.float32)).astype(jnp.float32)
    hit = first + second
    weight = first * upright(gates, 0) + second * upright(gates, 1)
    sub = lax.broadcasted_iota(jnp.int32, (8, META), 0)
    slot = jnp.zeros((8, META), jnp.float32)
    for t in range(7):
        slot = slot + jnp.where(sub > t, hit[t : t + 1, :], 0.0)
    slot = jnp.where(hit > 0.0, slot, -1.0)
    high = weight.astype(jnp.bfloat16).astype(jnp.float32)
    middle = (weight - high).astype(jnp.bfloat16).astype(jnp.float32)
    low = weight - high - middle
    routing = jnp.where(
        level == 0, high, jnp.where(level == 1, middle, jnp.where(level == 2, low, slot))
    )
    meta[0] = jnp.concatenate([routing, jnp.zeros_like(routing)], axis=0).astype(jnp.bfloat16)
    tokens = tok[...].astype(jnp.float32)
    stacked = jnp.concatenate([tokens[:, :half], tokens[:, half:]], axis=0)
    blocks[0] = stacked.astype(jnp.bfloat16)

    pl.semaphore_wait(barrier, 7)

    def send(source, target, peer, sem):
        copy = pltpu.make_async_remote_copy(
            src_ref=blocks.at[source],
            dst_ref=blocks.at[target],
            send_sem=gs_sem.at[sem],
            recv_sem=gr_sem.at[target],
            device_id=peer,
            device_id_type=MESH,
        )
        copy.start()
        return copy

    def arrived(index):
        pltpu.make_async_remote_copy(
            src_ref=blocks.at[index],
            dst_ref=blocks.at[index],
            send_sem=gs_sem.at[0],
            recv_sem=gr_sem.at[index],
            device_id=twin,
            device_id_type=MESH,
        ).wait_recv()

    sent = []
    def meta_copy(n, source, target, count, peer):
        return pltpu.make_async_remote_copy(
            src_ref=meta.at[pl.ds(source, count)],
            dst_ref=meta.at[pl.ds(target, count)],
            send_sem=ms_sem.at[n],
            recv_sem=mr_sem.at[n],
            device_id=peer,
            device_id_type=MESH,
        )

    meta_depth = [meta_copy(d - 1, 0, d, 1, depth[d]) for d in (1, 2, 3)]
    meta_column = [meta_copy(2 + g, 0, g * 4, 4, column[g]) for g in (1, 2, 3)]
    meta_twin = meta_copy(6, 0, 16, 16, twin)

    def to_twin(index):
        sent.append(send(index, 16 + index, twin, len(sent)))

    for copy in meta_depth:
        copy.start()
    order = (0, 2, 1, 3)
    for d in (2, 1, 3):
        sent.append(send(0, d, depth[d], len(sent)))
    for copy in meta_depth:
        copy.wait_recv()
    for copy in meta_column:
        copy.start()
    for d in order:
        if d:
            arrived(d)
        for g in (3, 1, 2) if d in (0, 2) else (1, 2):
            sent.append(send(d, g * 4 + d, column[g], len(sent)))
        to_twin(d)
    for copy in meta_column:
        copy.wait_recv()
    meta_twin.start()
    arrived(12)
    sent.append(send(12, 13, depth[1], len(sent)))
    to_twin(12)
    meta_twin.wait_recv()

    info = meta[...].astype(jnp.float32)[:, 0:8, :].reshape(total, META)
    lane = lax.broadcasted_iota(jnp.int32, (total, META), 1)
    mine = (lane % 32) == expert
    weight = jnp.sum(jnp.where(mine & (lane < 96), info, 0.0), axis=1, keepdims=True)
    slot = jnp.sum(jnp.where(mine & (lane >= 96), info, 0.0), axis=1, keepdims=True)
    place = lax.broadcasted_iota(jnp.int32, (total, total), 0)
    far_core = (core + place // 128) % 2
    far_x = (x + (place // 64) % 2) % 2
    far_y = (y + (place // 32) % 2) % 2
    far_z = ((z_high + (place // 16) % 2) % 2) * 2 + (z_low + (place // 8) % 2) % 2
    base = ((far_z * 2 + far_y) * 4 + far_x * 2 + far_core) * 8
    spot = lax.broadcasted_iota(jnp.int32, (total, total), 1) - base
    placing = (spot.astype(jnp.float32) == slot).astype(jnp.float32).T.astype(jnp.bfloat16)

    for copy in saved:
        copy.wait()
    for n in range(4):
        size = hidden // 4
        part = slice(n * size, (n + 1) * size)
        a = lax.dot_general(
            sgate_v[:, part], placing, LEADING, preferred_element_type=jnp.float32
        )
        b = lax.dot_general(sup_v[:, part], placing, LEADING, preferred_element_type=jnp.float32)
        q = jax.nn.sigmoid(a)
        up_f[part, :] = a * q
        gate_f[part, :] = b * q * (1.0 + a * (1.0 - q))
        for g in (1, 2):
            arrived(g * 4 + order[n])
            to_twin(g * 4 + order[n])
        if n == 0:
            arrived(14)
            sent.append(send(14, 15, depth[1], len(sent)))
            to_twin(14)
    for d in (1, 3):
        arrived(12 + d)
        to_twin(12 + d)

    quarter = half // 4
    for k in range(2):
        if k == 1:
            for index in range(16, 32):
                arrived(index)
        span = slice(k * 128, (k + 1) * 128)
        for n in range(4):
            part = blocks[k * 16 : k * 16 + 16, :, n * quarter : (n + 1) * quarter]
            part = part.astype(jnp.float32)
            for h in range(2):
                value = part[:, h * 8 : h * 8 + 8, :].reshape(128, quarter) * weight[span]
                start = h * half + n * quarter
                rows[start : start + quarter, span] = value.astype(jnp.bfloat16).T

    @pl.loop(0, hidden_steps)
    def _(n):
        down_copy(n).wait()
        part = pl.ds(pl.multiple_of(n * CHUNK, CHUNK), CHUNK)
        grad = jnp.dot(down_v[part, :], rows[...], preferred_element_type=jnp.float32)
        up_g[part, :] = (grad * up_f[part, :]).astype(jnp.bfloat16)
        gate_g[part, :] = (grad * gate_f[part, :]).astype(jnp.bfloat16)

    def a_copy(j):
        return pltpu.make_async_remote_copy(
            src_ref=a_send.at[j],
            dst_ref=a_recv.at[j],
            send_sem=as_sem.at[j],
            recv_sem=ar_sem.at[j],
            device_id=twin,
            device_id_type=MESH,
        )

    def b_copy(j, leg):
        along_y = (j + leg) % 2
        peer = (((x + 1 - along_y) % 2) * 2 + core, z * 2 + (y + along_y) % 2)
        part = pl.ds(0, 64) if leg == 0 else pl.ds(64, 32)
        return pltpu.make_async_remote_copy(
            src_ref=b_send.at[j, part],
            dst_ref=b_recv.at[j, part],
            send_sem=bs_sem.at[j, leg],
            recv_sem=br_sem.at[j, leg],
            device_id=peer,
            device_id_type=MESH,
        )

    def c_copy(j, d):
        return pltpu.make_async_remote_copy(
            src_ref=c_send.at[j, d - 1],
            dst_ref=c_recv.at[j, d - 1],
            send_sem=cs_sem.at[j, d - 1],
            recv_sem=cr_sem.at[j, d - 1],
            device_id=depth[d],
            device_id_type=MESH,
        )

    @pl.loop(0, steps + 5)
    def _(i):
        @pl.when(i < steps)
        def _():
            gate_copy(i).wait()
            up_copy(i).wait()
            part = pl.ds(pl.multiple_of(i * CHUNK, CHUNK), CHUNK)
            value = jnp.dot(
                gate_v[part, :], gate_g[...], preferred_element_type=jnp.float32
            ) + jnp.dot(up_v[part, :], up_g[...], preferred_element_type=jnp.float32)
            a_send[i] = value[:, 128:256].astype(jnp.bfloat16)
            a_copy(i).start()
            own[i] = value[:, 0:128]

        @pl.when((i >= 1) & (i < steps + 1))
        def _():
            j = i - 1
            a_copy(j).wait_recv()
            value = (own[j] + a_recv[j].astype(jnp.float32)).T
            odd = (j % 2) == 1
            along_y, along_x = value[32:64], value[64:96]
            b_send[j, 0:32, :] = jnp.where(odd, along_y, along_x).astype(jnp.bfloat16)
            b_send[j, 32:64, :] = value[96:128].astype(jnp.bfloat16)
            b_copy(j, 0).start()
            col[j, 0:32, :] = value[0:32]
            col[j, 32:64, :] = jnp.where(odd, along_x, along_y)

        @pl.when((i >= 3) & (i < steps + 3))
        def _():
            j = i - 3
            b_copy(j, 0).wait_recv()
            value = col[j] + b_recv[j, 0:64, :].astype(jnp.float32)
            b_send[j, 64:96, :] = value[32:64].astype(jnp.bfloat16)
            b_copy(j, 1).start()
            col[j, 0:32, :] = value[0:32]

        @pl.when((i >= 4) & (i < steps + 4))
        def _():
            j = i - 4
            b_copy(j, 1).wait_recv()
            value = col[j, 0:32, :] + b_recv[j, 64:96, :].astype(jnp.float32)
            for d in (2, 1, 3):
                line = value[d * 8 : d * 8 + 8]
                folded = jnp.concatenate([line[:, : CHUNK // 2], line[:, CHUNK // 2 :]], axis=0)
                c_send[j, d - 1] = folded.astype(jnp.bfloat16)
                c_copy(j, d).start()
            col[j, 0:8, :] = value[0:8]

        @pl.when(i >= 5)
        def _():
            j = i - 5
            value = col[j, 0:8, :]
            for d in (1, 2, 3):
                c_copy(j, d).wait_recv()
                folded = c_recv[j, d - 1].astype(jnp.float32)
                value = value + jnp.concatenate([folded[0:8], folded[8:16]], axis=1)
            part = pl.ds(pl.multiple_of(j * CHUNK, CHUNK), CHUNK)
            out[:, part] = value.astype(out.dtype)

    for copy in sent + meta_depth + meta_column + [meta_twin]:
        copy.wait_send()

    @pl.loop(0, steps)
    def _(j):
        a_copy(j).wait_send()
        for leg in (0, 1):
            b_copy(j, leg).wait_send()
        for d in (1, 2, 3):
            c_copy(j, d).wait_send()


def fused_shards(out_grad, routes, gate_weight, gate_proj, up_proj, down_proj, saved_gate, saved_up):
    feature = out_grad.shape[1]
    hidden = gate_proj.shape[2]
    total = saved_gate.shape[1]
    steps = feature // CHUNK
    bf16, f32 = jnp.bfloat16, jnp.float32
    vmem = pl.BlockSpec(memory_space=pltpu.VMEM)
    anywhere = pl.BlockSpec(memory_space=pl.ANY)
    dma = pltpu.SemaphoreType.DMA
    flops = 2 * 3 * total * feature * hidden
    return pl.pallas_call(
        fused_kernel,
        out_shape=jax.ShapeDtypeStruct(out_grad.shape, bf16),
        in_specs=[vmem] * 3 + [anywhere] * 5,
        out_specs=vmem,
        scratch_shapes=[
            pltpu.VMEM((feature, hidden), bf16),
            pltpu.VMEM((feature, hidden), bf16),
            pltpu.VMEM((hidden, feature), bf16),
            pltpu.VMEM((total, hidden), bf16),
            pltpu.VMEM((total, hidden), bf16),
            pltpu.VMEM((32, 16, feature // 2), bf16),
            pltpu.VMEM((32, 16, META), bf16),
            pltpu.VMEM((feature, total), bf16),
            pltpu.VMEM((hidden, total), bf16),
            pltpu.VMEM((hidden, total), bf16),
            pltpu.VMEM((hidden, total), f32),
            pltpu.VMEM((hidden, total), f32),
            pltpu.VMEM((steps, CHUNK, 128), f32),
            pltpu.VMEM((steps, CHUNK, 128), bf16),
            pltpu.VMEM((steps, CHUNK, 128), bf16),
            pltpu.VMEM((steps, 64, CHUNK), f32),
            pltpu.VMEM((steps, 96, CHUNK), bf16),
            pltpu.VMEM((steps, 96, CHUNK), bf16),
            pltpu.VMEM((steps, 3, 16, CHUNK // 2), bf16),
            pltpu.VMEM((steps, 3, 16, CHUNK // 2), bf16),
            dma((3, max(steps, hidden // CHUNK))),
            dma((2,)),
            dma((7,)),
            dma((7,)),
            dma((31,)),
            dma((32,)),
            dma((steps,)),
            dma((steps,)),
            dma((steps, 2)),
            dma((steps, 2)),
            dma((steps, 3)),
            dma((steps, 3)),
        ],
        compiler_params=pltpu.CompilerParams(
            collective_id=0, has_side_effects=True, vmem_limit_bytes=60 * 1024 * 1024
        ),
        cost_estimate=pl.CostEstimate(
            flops=flops, bytes_accessed=3 * 2 * feature * hidden, transcendentals=total * hidden
        ),
    )(out_grad, routes.T, gate_weight.T, gate_proj, up_proj, down_proj, saved_gate, saved_up)


def rank_slots(flat_routes):
    count = flat_routes.shape[-1]
    positions = jnp.arange(count, dtype=jnp.int32)
    before = positions[:, None] < positions[None, :]
    matches = flat_routes[..., :, None] == flat_routes[..., None, :]
    return jnp.sum(jnp.logical_and(matches, before), axis=-2)


def expert_rows(grad_rows, gate_mat, up_mat, down_mat, pre_gate, pre_up):
    contract = (((1,), (1,)), ((), ()))
    hidden_grad = lax.dot_general(grad_rows, down_mat, contract, preferred_element_type=jnp.float32)
    gate_vals = pre_gate.astype(jnp.float32)
    up_vals = pre_up.astype(jnp.float32)
    sigmoid_gate = jax.nn.sigmoid(gate_vals)
    up_grad = (hidden_grad * gate_vals * sigmoid_gate).astype(jnp.bfloat16)
    gate_grad = (
        hidden_grad * up_vals * sigmoid_gate * (1.0 + gate_vals * (1.0 - sigmoid_gate))
    ).astype(jnp.bfloat16)
    partial_value = lax.dot_general(
        gate_grad, gate_mat, contract, preferred_element_type=jnp.float32
    )
    return partial_value + lax.dot_general(
        up_grad, up_mat, contract, preferred_element_type=jnp.float32
    )


def shards(out_grad, routes, gate_weight, gate_proj, up_proj, down_proj, saved_gate, saved_up):
    expert_count = lax.axis_size("expert")
    cut_count = lax.axis_size("cuts")
    tok_rows = out_grad.shape[0]
    feature_dim = out_grad.shape[1]
    slot_count = saved_gate.shape[1] // (expert_count * cut_count)
    flat_routes = routes.reshape(-1)
    slot_index = rank_slots(flat_routes[None, :])[0]
    own_spots = flat_routes * slot_count + slot_index
    routed = (gate_weight[:, :, None] * out_grad.astype(jnp.float32)[:, None, :]).astype(
        jnp.bfloat16
    )
    routed = routed.reshape(2 * tok_rows, feature_dim)
    places = jnp.arange(expert_count * slot_count, dtype=jnp.int32)
    placing = (places[:, None] == own_spots[None, :]).astype(jnp.bfloat16)
    outgoing = jnp.dot(placing, routed, preferred_element_type=jnp.float32).astype(jnp.bfloat16)
    outgoing = outgoing.reshape(expert_count, slot_count, feature_dim)
    arrived = lax.all_to_all(outgoing, "expert", split_axis=0, concat_axis=0, tiled=True)
    gathered = lax.all_gather(arrived, "cuts", axis=0, tiled=True).reshape(-1, feature_dim)
    gate_block = saved_gate[0]
    up_block = saved_up[0]
    own_rows = lax.psum_scatter(
        expert_rows(gathered, gate_proj[0], up_proj[0], down_proj[0], gate_block, up_block),
        "cuts",
        scatter_dimension=0,
        tiled=True,
    )
    own_rows = own_rows.reshape(expert_count, slot_count, feature_dim)
    returned = lax.all_to_all(own_rows, "expert", split_axis=0, concat_axis=0, tiled=True).reshape(
        -1, feature_dim
    )
    picked = returned[own_spots].reshape(tok_rows, 2, feature_dim)
    summed = jnp.sum(picked, axis=1)
    return summed.astype(jnp.bfloat16)


def solution(mesh):
    in_specs = (
        P(("expert", "cuts"), None),
        P(("expert", "cuts"), None),
        P(("expert", "cuts"), None),
        P("expert", None, "cuts"),
        P("expert", None, "cuts"),
        P("expert", "cuts", None),
        P("expert", None, "cuts"),
        P("expert", None, "cuts"),
    )
    out_specs = P(("expert", "cuts"), None)
    fused = (mesh.shape["expert"], mesh.shape["cuts"]) == (4, 8)
    body = fused_shards if fused else shards
    return jax.shard_map(body, mesh=mesh, in_specs=in_specs, out_specs=out_specs, check_vma=False)
```
